32 devices in a mesh: fsdp: 16 (over z, x, core), seq: 2 (over y).
Axes of the slice: x: 2, y: 2, z: 4, core: 2. Of those that a mesh axis runs over, the one named last changes fastest.
Arguments:
- tokens: bfloat16 [16, 1024, 1024], P('fsdp', 'seq'), may hold values from -6 to 6
- positions: int32 [3, 16, 1024], P(None, 'fsdp', 'seq'), may hold values from 0 to 15
- ln1_gain: bfloat16 [1024], P('fsdp'), may hold values from 0.099609375 to 1.8984375
- ln1_bias: bfloat16 [1024], P('fsdp'), may hold values from -3 to 3
- qkv_weight: bfloat16 [1024, 3072], P('fsdp'), may hold values from -0.1875 to 0.1875
- qkv_bias: bfloat16 [3072], P('fsdp'), may hold values from -0.19921875 to 0.19921875
- out_weight: bfloat16 [1024, 1024], P('fsdp'), may hold values from -4 to 4
- out_bias: bfloat16 [1024], P('fsdp'), may hold values from -3 to 3
- ln2_gain: bfloat16 [1024], P('fsdp'), may hold values from 0.099609375 to 1.8984375
- ln2_bias: bfloat16 [1024], P('fsdp'), may hold values from -3 to 3
- fc1_weight: bfloat16 [1024, 4096], P('fsdp'), may hold values from -0.1875 to 0.1875
- fc1_bias: bfloat16 [4096], P('fsdp'), may hold values from -3 to 3
- fc2_weight: bfloat16 [4096, 1024], P('fsdp'), may hold values from -0.09375 to 0.09375
- fc2_bias: bfloat16 [1024], P('fsdp'), may hold values from -3 to 3
- out_grad: bfloat16 [16, 1024, 1024], P('fsdp', 'seq'), may hold values from -6 to 6
Outputs:
- block_out: bfloat16 [16, 1024, 1024], P('fsdp', 'seq')
- tokens_grad: float32 [16, 1024, 1024], P('fsdp', 'seq')
- ln1_gain_grad: float32 [1024], P('fsdp')
- ln1_bias_grad: float32 [1024], P('fsdp')
- qkv_weight_grad: float32 [1024, 3072], P('fsdp')
- qkv_bias_grad: float32 [3072], P('fsdp')
- out_weight_grad: float32 [1024, 1024], P('fsdp')
- out_bias_grad: float32 [1024], P('fsdp')
- ln2_gain_grad: float32 [1024], P('fsdp')
- ln2_bias_grad: float32 [1024], P('fsdp')
- fc1_weight_grad: float32 [1024, 4096], P('fsdp')
- fc1_bias_grad: float32 [4096], P('fsdp')
- fc2_weight_grad: float32 [4096, 1024], P('fsdp')
- fc2_bias_grad: float32 [1024], P('fsdp')
The draws below stay inside these ranges and needn't reach their ends.
All inputs are finite; a program needn't handle non-finite values.
Results may differ from the reference program's by a relative error of at most 0.011.
Values may be sent and summed in bfloat16 or wider, within the bound.
No kernel may reach another device: no remote copies, remote signals or barrier semaphores. Data moves between devices by JAX's collectives and lax.ppermute only.
A program may use at most 192 MiB of HBM per device.

```python
import jax
import jax.numpy as jnp
from jax import lax

D = 1024
HEADS = 16
FF = 4096
HD = 64
GRID = 16
CLIP = 1024
CLIPS = 16


def plant(entries, stream_key, least, high):
    longest = entries.shape.index(max(entries.shape))
    spots = []
    for shift in (0, 1):
        where = [jax.random.randint(jax.random.fold_in(stream_key, axis), (), 0, length) for axis, length in enumerate(entries.shape)]
        where[longest] = (where[longest] + shift) % entries.shape[longest]
        spots.append(tuple(where))
    return entries.at[spots[0]].set(least).at[spots[1]].set(high)


def strengthened(values, rng, source, target, blocks, factor):
    owner, partner = [(jnp.arange(values.shape[dim]) // (values.shape[dim] // blocks)).reshape([-1 if axis == dim else 1 for axis in range(values.ndim)]) for dim in (source, target)]
    chosen = jax.random.permutation(rng, blocks)[partner]
    strong = (owner == chosen) | (owner == (partner + blocks // 2) % blocks)
    return jnp.where(strong, factor * values, values)


def level_of(rng, extent, shards, low, high):
    def one(axis_at, blocks):
        draws = jax.random.uniform(jax.random.fold_in(jax.random.fold_in(rng, 6), axis_at), (blocks,), jnp.float32, low / len(shards), high / len(shards))
        return jnp.repeat(jnp.exp(draws), extent[axis_at] // blocks).reshape((-1,) + (1,) * (len(extent) - axis_at - 1))

    loudness = one(*shards[0])
    for cut in shards[1:]:
        loudness = loudness * one(*cut)
    return loudness


def normal_values(stream_key, dims, deviation, reach, cuts=(), held_as=jnp.bfloat16):
    values = jax.random.normal(stream_key, dims, jnp.float32) * deviation
    if len(cuts) > 0:
        values = level_of(stream_key, dims, cuts, -0.22, 0.18) * values
    return jnp.clip(values, min=-reach, max=reach).astype(held_as)


def gaussian_with(stream_key, extent, scale, most, split, heavy, held_as=jnp.bfloat16):
    values = scale * jax.random.normal(stream_key, extent, jnp.float32)
    if split:
        values = values * level_of(stream_key, extent, split, -0.22, 0.18)
    return jnp.clip(strengthened(values, jax.random.fold_in(stream_key, 3), *heavy), -most, most).astype(held_as)


def setup_inputs(seed: int = 0) -> dict:
    key_of = jax.random.split(jax.random.key(seed), 16)
    tokens = normal_values(key_of[0], (CLIPS, CLIP, D), 1.0, 6.0, ((0, 16), (1, 2)))
    positions = plant(jax.random.randint(key_of[1], (3, CLIPS, CLIP), 0, GRID), jax.random.fold_in(key_of[1], 1), 0, GRID - 1).astype(jnp.int32)
    ln1_gain = jnp.clip(1.0 + 0.18 * jax.random.normal(key_of[2], (D,), jnp.float32), 0.099609375, 1.8984375).astype(jnp.bfloat16)
    ln1_bias = normal_values(key_of[3], (D,), 0.5, 3.0, ((0, 16),))
    qkv_weight = normal_values(key_of[4], (D, 3 * D), D ** -0.5, 0.1875, ((0, 16),))
    qkv_bias = normal_values(key_of[5], (3 * D,), 0.03, 0.19921875, ((0, 16),))
    out_weight = normal_values(key_of[6], (D, D), 0.8, 4.0, ((0, 16),))
    out_bias = normal_values(key_of[7], (D,), 0.5, 3.0, ((0, 16),))
    ln2_gain = jnp.clip(1.0 + 0.18 * jax.random.normal(key_of[8], (D,), jnp.float32), 0.099609375, 1.8984375).astype(jnp.bfloat16)
    ln2_bias = normal_values(key_of[9], (D,), 0.5, 3.0, ((0, 16),))
    fc1_weight = normal_values(key_of[10], (D, FF), D ** -0.5, 0.1875, ((0, 16),))
    fc1_bias = normal_values(key_of[11], (FF,), 0.5, 3.0, ((0, 16),))
    fc2_weight = normal_values(key_of[12], (FF, D), FF ** -0.5, 0.09375, ((0, 16),))
    fc2_bias = normal_values(key_of[13], (D,), 0.5, 3.0, ((0, 16),))
    out_grad = gaussian_with(key_of[14], (CLIPS, CLIP, D), 1.0, 6.0, ((0, 16), (1, 2)), (0, 2, 16, 2.0))
    return dict(tokens=tokens, positions=positions, ln1_gain=ln1_gain, ln1_bias=ln1_bias, qkv_weight=qkv_weight, qkv_bias=qkv_bias, out_weight=out_weight, out_bias=out_bias, ln2_gain=ln2_gain, ln2_bias=ln2_bias, fc1_weight=fc1_weight, fc1_bias=fc1_bias, fc2_weight=fc2_weight, fc2_bias=fc2_bias, out_grad=out_grad)


@jax.custom_vjp
def low(v):
    return lax.optimization_barrier(v.astype(jnp.bfloat16)).astype(jnp.float32)

@jax.custom_vjp
def low_back(v):
    return v

def low_keep(v):
    return (low(v), None)

def low_pass(kept, grad):
    return (grad,)

def back_keep(v):
    return (v, None)

def back_low(kept, grad):
    return (low(grad),)
low.defvjp(low_keep, low_pass)
low_back.defvjp(back_keep, back_low)
eps_norm = 1e-06
theta_base = 10000.0
highest = lax.Precision.HIGHEST

def layer_norm(values, gain, shift):
    center = values - lax.optimization_barrier(jnp.mean(values, axis=-1, keepdims=True))
    spread = lax.optimization_barrier(jnp.mean(center * center, axis=-1, keepdims=True))
    return center * lax.rsqrt(spread + eps_norm) * gain + shift

def gelu_exact(values):
    return 0.5 * values * (1.0 + lax.erf(values * 0.7071067811865476))

def rotary_tables(index_rows, head_dim):
    rot_width = 2 * (head_dim // 3 // 2)
    half_width = rot_width // 2
    exponent = jnp.arange(half_width).astype(jnp.float32) * (2.0 / rot_width)
    freqs = jnp.power(jnp.float32(theta_base), -exponent)
    angles = index_rows.astype(jnp.float32)[:, :, None] * freqs
    return (jnp.cos(angles), jnp.sin(angles))

def rotate(values, cosines, sines):
    half_width = cosines.shape[-1]
    rot_width = 2 * half_width
    pieces = []
    for axis_number in range(3):
        offset = axis_number * rot_width
        leading = values[:, :, offset:offset + half_width]
        trailing = values[:, :, offset + half_width:offset + rot_width]
        cosine_part = cosines[axis_number][:, None, :]
        sine_part = sines[axis_number][:, None, :]
        pieces.append(leading * cosine_part - trailing * sine_part)
        pieces.append(trailing * cosine_part + leading * sine_part)
    pieces.append(values[:, :, 3 * rot_width:])
    return jnp.concatenate(pieces, axis=-1)

def matmul(left, right):
    return jnp.dot(left, right, precision=highest, preferred_element_type=jnp.float32)

def attend_block(query_block, keys, values_all):
    scale = HD ** (-0.5)
    scores = jnp.einsum('qhd,khd->hqk', query_block, keys, precision=highest) * scale
    scores = low_back(scores)
    peak = lax.optimization_barrier(jnp.max(scores, axis=-1, keepdims=True))
    weights = jnp.exp(scores - peak)
    probs = low(weights / lax.optimization_barrier(jnp.sum(weights, axis=-1, keepdims=True)))
    return jnp.einsum('hqk,khd->qhd', probs, values_all, precision=highest)

def forward(tokens_f, params, cosines, sines):
    gain_one, bias_one, w_qkv, b_qkv, w_out, b_out, gain_two, bias_two, w_up, b_up, w_down, b_down = params
    rows = tokens_f.shape[0]
    normed_one = low(layer_norm(tokens_f, gain_one, bias_one))
    mixed = low_back(matmul(normed_one, w_qkv) + b_qkv)
    queries = mixed[:, :D].reshape(rows, HEADS, HD)
    keys = mixed[:, D:2 * D].reshape(rows, HEADS, HD)
    values_all = mixed[:, 2 * D:].reshape(rows, HEADS, HD)
    queries = low(low_back(rotate(queries, cosines, sines)))
    keys = low(low_back(rotate(keys, cosines, sines)))
    values_all = low(low_back(values_all))
    block = min(512, rows)
    count = rows // block
    checked = jax.checkpoint(attend_block)
    attended = lax.map(lambda query_block: checked(query_block, keys, values_all), queries.reshape(count, block, HEADS, HD))
    attended = low(low_back(attended.reshape(rows, D)))
    hidden = tokens_f + low_back(matmul(attended, w_out) + b_out)
    normed_two = low(layer_norm(hidden, gain_two, bias_two))
    preact = low_back(matmul(normed_two, w_up) + b_up)
    activated = low(gelu_exact(preact))
    return hidden + matmul(activated, w_down) + b_down

def reference(tokens, positions, ln1_gain, ln1_bias, qkv_weight, qkv_bias, out_weight, out_bias, ln2_gain, ln2_bias, fc1_weight, fc1_bias, fc2_weight, fc2_bias, out_grad):
    params = tuple([weight.astype(jnp.float32) for weight in (ln1_gain, ln1_bias, qkv_weight, qkv_bias, out_weight, out_bias, ln2_gain, ln2_bias, fc1_weight, fc1_bias, fc2_weight, fc2_bias)])

    def per_clip(totals, inputs):
        clip_tokens, clip_positions, clip_grad = inputs
        cosines, sines = rotary_tables(clip_positions, HD)

        def run(tokens_f, weights):
            return forward(tokens_f, weights, cosines, sines)
        result, pullback = jax.vjp(run, clip_tokens.astype(jnp.float32), params)
        token_part, weight_parts = pullback(clip_grad.astype(jnp.float32))
        totals = tuple([total + part for total, part in zip(totals, weight_parts)])
        return (totals, (result.astype(jnp.bfloat16), token_part))
    zeros_all = tuple([jnp.zeros(weight.shape, jnp.float32) for weight in params])
    clip_positions = jnp.moveaxis(positions, 1, 0)
    totals, outputs = lax.scan(per_clip, zeros_all, (tokens, clip_positions, out_grad))
    return (outputs[0], outputs[1], totals[0], totals[1], totals[2], totals[3], totals[4], totals[5], totals[6], totals[7], totals[8], totals[9], totals[10], totals[11])
```

```python
import functools

import jax
import jax.numpy as jnp
import numpy as np
from jax import lax
from jax.experimental import pallas as pl
from jax.experimental.pallas import tpu as pltpu
from jax.sharding import PartitionSpec as P

HD = 64
EPS = 1e-06
THETA = 10000.0
LOG2E = 1.4426950408889634
SCALE = HD**-0.5
BF = jnp.bfloat16
F32 = jnp.float32
NT = (((1,), (1,)), ((), ()))
TN = (((0,), (0,)), ((), ()))
NN = (((1,), (0,)), ((), ()))
SMALL = 128
VMEM_BYTES = 56 << 20
SHARD = "fsdp"
SEQ = "seq"


def mm(a, b, dims=NN):
    return lax.dot_general(a, b, dims, preferred_element_type=F32)


def shifted(size, by):
    return [(i, (i + by) % size) for i in range(size)]


def take(values, index, axis):
    return lax.dynamic_index_in_dim(values, index, axis, keepdims=False)


def shape(dims, dtype):
    return jax.ShapeDtypeStruct(dims, dtype)


def fixed(*dims):
    return pl.BlockSpec(dims, lambda *_: (0,) * len(dims))


def call(kernel, grid, in_specs, out_specs, out_shape, flops, moved, exps=0, scratch=()):
    return pl.pallas_call(
        kernel,
        grid=grid,
        in_specs=in_specs,
        out_specs=out_specs,
        out_shape=out_shape,
        scratch_shapes=list(scratch),
        compiler_params=pltpu.CompilerParams(vmem_limit_bytes=VMEM_BYTES),
        cost_estimate=pl.CostEstimate(flops=flops, bytes_accessed=moved, transcendentals=exps),
    )


def rotated(values, cos, low, high):
    half = 2 * (HD // 3 // 2) // 2
    return values * cos + pltpu.roll(values, values.shape[1] - half, 1) * low + pltpu.roll(values, half, 1) * high


def project_kernel(x_ref, w_ref, b_ref, cos_ref, low_ref, high_ref, out_ref):
    values = mm(x_ref[...], w_ref[...]) + b_ref[...]
    width = values.shape[1]

    @pl.when(pl.program_id(0) < 2)
    def _():
        cos, low, high = cos_ref[...], low_ref[...], high_ref[...]
        for j in range(0, width, 128):
            out_ref[:, j : j + 128] = rotated(values[:, j : j + 128], cos, low, high).astype(BF)

    @pl.when(pl.program_id(0) >= 2)
    def _():
        out_ref[...] = values.astype(BF)


def project(x, weight, bias, tables, width):
    rows, depth = x.shape
    start = depth // width
    return call(
        project_kernel,
        (3,),
        [
            fixed(rows, depth),
            pl.BlockSpec((depth, width), lambda i: (0, start + i)),
            pl.BlockSpec((1, width), lambda i: (0, i)),
        ]
        + [fixed(rows, 128)] * 3,
        pl.BlockSpec((rows, width), lambda i: (0, i)),
        shape((rows, 3 * width), BF),
        6 * rows * depth * width,
        6 * depth * width + 2 * rows * (depth + 3 * width),
    )(x, weight, bias, *tables)


def rotary_tables(positions):
    width = 2 * (HD // 3 // 2)
    half = width // 2
    freqs = np.power(np.float32(THETA), -(np.arange(half, dtype=np.float32) * np.float32(2.0 / width)))
    column = np.arange(2 * HD) % HD
    turns = column < 3 * width
    axis = np.minimum(column // width, 2)
    freq = np.where(turns, freqs[column % half], 0.0).astype(np.float32)
    leading = turns & (column % width < half)
    trailing = turns & (column % width >= half)
    place = jnp.where(axis == 0, positions[0][:, None], jnp.where(axis == 1, positions[1][:, None], positions[2][:, None]))
    angle = place * freq
    sine = jnp.sin(angle)
    return jnp.cos(angle), jnp.where(leading, -sine, 0.0), jnp.where(trailing, sine, 0.0)


def over_blocks(rows, block, step):
    if rows // block <= 4:
        for i in range(rows // block):
            step(pl.ds(i * block, block))
    else:

        def body(i, carry):
            step(pl.ds(pl.multiple_of(i * block, block), block))
            return carry

        lax.fori_loop(0, rows // block, body, 0)


def attend_kernel(block, q_ref, k_ref, v_ref, o_ref, lse_ref):
    rows = q_ref.shape[0]
    first = lax.broadcasted_iota(jnp.int32, (1, 128), 1) < HD
    factor = jnp.float32(SCALE * LOG2E)
    zero = jnp.zeros((), BF)

    def step(rs):
        q = q_ref[rs, :]
        outs, lses = [], []
        for h in range(2):
            mine = first if h == 0 else jnp.logical_not(first)
            scores = mm(jnp.where(mine, q, zero), k_ref[...], NT)
            peak = jnp.max(scores, axis=1, keepdims=True) * factor
            weights = jnp.exp2(scores * factor - peak)
            total = jnp.sum(weights, axis=1, keepdims=True)
            outs.append(mm(weights.astype(BF), v_ref[...]) * (1.0 / total))
            lses.append(peak + jnp.log2(total))
        o_ref[rs, :] = jnp.where(first, outs[0], outs[1]).astype(BF)
        lse_ref[rs, :] = jnp.where(first, lses[0], lses[1])

    over_blocks(rows, block, step)


def attend_back_kernel(
    block, q_ref, k_ref, v_ref, o_ref, lse_ref, do_ref, cos_ref, low_ref, high_ref, dq_ref, dk_ref, dv_ref, dk_sum, dv_sum
):
    rows = q_ref.shape[0]
    first = lax.broadcasted_iota(jnp.int32, (1, 128), 1) < HD
    factor = jnp.float32(SCALE * LOG2E)
    zero = jnp.zeros((), BF)
    dk_sum[...] = jnp.zeros_like(dk_sum)
    dv_sum[...] = jnp.zeros_like(dv_sum)

    def step(rs):
        q, do = q_ref[rs, :], do_ref[rs, :]
        od = o_ref[rs, :].astype(F32) * do.astype(F32)
        lse = lse_ref[rs, :]
        dq = None
        for h in range(2):
            mine = first if h == 0 else jnp.logical_not(first)
            qh, doh = jnp.where(mine, q, zero), jnp.where(mine, do, zero)
            delta = jnp.sum(jnp.where(mine, od, 0.0), axis=1, keepdims=True)
            k = k_ref[...]
            p = jnp.exp2(mm(qh, k, NT) * factor - lse[:, h * HD : h * HD + 1])
            ds = (p * (mm(doh, v_ref[...], NT) - delta)).astype(BF)
            dv_sum[...] += mm(p.astype(BF), doh, TN)
            dk_sum[...] += mm(ds, qh, TN)
            part = mm(ds, jnp.where(mine, k, zero))
            dq = part if dq is None else dq + part
        dq = (dq * SCALE).astype(BF).astype(F32)
        dq_ref[rs, :] = rotated(dq, cos_ref[rs, :], -low_ref[rs, :], -high_ref[rs, :]).astype(BF)

    over_blocks(rows, block, step)
    dk = (dk_sum[...] * SCALE).astype(BF).astype(F32)
    dk_ref[...] = rotated(dk, cos_ref[...], -low_ref[...], -high_ref[...]).astype(BF)
    dv_ref[...] = dv_sum[...].astype(BF)


def pair_spec(rows, first=0):
    return pl.BlockSpec((rows, 128), lambda i: (0, first + i))


def attend(qkv, block=512):
    rows, columns = qkv.shape[0], qkv.shape[1] // 3
    pairs = columns // 128
    return call(
        functools.partial(attend_kernel, min(block, (1 << 19) // rows)),
        (pairs,),
        [pair_spec(rows, k * pairs) for k in range(3)],
        [pair_spec(rows)] * 2,
        [shape((rows, columns), BF), shape((rows, columns), F32)],
        16 * rows * rows * columns,
        rows * columns * 12,
        rows * rows * columns // HD,
    )(qkv, qkv, qkv)


def attend_back(qkv, o, lse, do, tables, block=512):
    rows, columns = o.shape
    pairs = columns // 128
    return call(
        functools.partial(attend_back_kernel, min(block, (1 << 19) // rows)),
        (pairs,),
        [pair_spec(rows, k * pairs) for k in range(3)] + [pair_spec(rows)] * 3 + [fixed(rows, 128)] * 3,
        [pair_spec(rows)] * 3,
        [shape((rows, columns), BF)] * 3,
        40 * rows * rows * columns,
        rows * columns * 20,
        rows * rows * columns // HD,
        [pltpu.VMEM((rows, 128), F32)] * 2,
    )(qkv, qkv, qkv, o, lse, do, *tables)


def normalise(values):
    center = values - jnp.mean(values, axis=-1, keepdims=True)
    factor = lax.rsqrt(jnp.mean(center * center, axis=-1, keepdims=True) + EPS)
    return center * factor, factor


def normalise_back(grads, gain, normal, factor):
    e = grads * gain
    inner = e - jnp.mean(e, axis=-1, keepdims=True) - normal * jnp.mean(e * normal, axis=-1, keepdims=True)
    return factor * inner


def column_sums(out_ref, *parts):
    sums = [jnp.sum(p, axis=0, keepdims=True) for p in parts]
    sums.append(jnp.zeros((8 - len(sums), sums[0].shape[1]), F32))
    block = jnp.concatenate(sums, axis=0)

    @pl.when(pl.program_id(0) == 0)
    def _():
        out_ref[...] = block

    @pl.when(pl.program_id(0) > 0)
    def _():
        out_ref[...] += block


def out_kernel(att_ref, w_ref, tokens_ref, b_ref, gain_ref, bias_ref, hidden_ref, normed_ref):
    hidden = tokens_ref[...].astype(F32) + mm(att_ref[...], w_ref[...]) + b_ref[...]
    hidden_ref[...] = hidden
    normed_ref[...] = (normalise(hidden)[0] * gain_ref[...] + bias_ref[...]).astype(BF)


def project_out(att, weight, tokens, b, gain, bias, block=256):
    rows, width = tokens.shape
    row = pl.BlockSpec((block, width), lambda i: (i, 0))
    return call(
        out_kernel,
        (rows // block,),
        [row, fixed(width, width), row] + [fixed(1, width)] * 3,
        [row, row],
        [shape((rows, width), F32), shape((rows, width), BF)],
        2 * rows * width * width,
        2 * width * width + 10 * rows * width,
    )(att, weight, tokens, b, gain, bias)


def hidden_back_kernel(extra, *refs):
    dn_ref, far_refs, (hidden_ref, og_ref, gain_ref, w_ref, grad_ref, branch_ref, att_ref, sums_ref) = (
        refs[0],
        refs[1 : 1 + extra],
        refs[1 + extra :],
    )
    dn = dn_ref[...]
    for far in far_refs:
        dn = dn + far[...].astype(F32)
    normal, factor = normalise(hidden_ref[...])
    og = og_ref[...].astype(F32)
    grad = og + normalise_back(dn, gain_ref[...], normal, factor)
    grad_ref[...] = grad
    branch = grad.astype(BF)
    branch_ref[...] = branch
    att_ref[...] = mm(branch, w_ref[...], NT).astype(BF)
    column_sums(sums_ref, dn * normal, dn, branch.astype(F32), og)


def hidden_back(dn, dn_far, hidden, og, gain, weight, block=256):
    rows, width = hidden.shape
    row = pl.BlockSpec((block, width), lambda i: (i, 0))
    return call(
        functools.partial(hidden_back_kernel, len(dn_far)),
        (rows // block,),
        [row] * (1 + len(dn_far)) + [row, row, fixed(1, width), fixed(width, width)],
        [row, row, row, fixed(8, width)],
        [shape((rows, width), F32), shape((rows, width), BF), shape((rows, width), BF), shape((8, width), F32)],
        2 * rows * width * width,
        2 * width * width + 18 * rows * width,
    )(dn, *dn_far, hidden, og, gain, weight)


def tokens_back_kernel(extra, *refs):
    dn_ref, far_refs, (tokens_ref, grad_ref, gain_ref, out_ref) = refs[0], refs[1 : 1 + extra], refs[1 + extra :]
    dn = dn_ref[...]
    for far in far_refs:
        dn = dn + far[...].astype(F32)
    normal, factor = normalise(tokens_ref[...].astype(F32))
    out_ref[...] = grad_ref[...] + normalise_back(dn, gain_ref[...], normal, factor)


def tokens_back(dn, dn_far, tokens, grad, gain, block=256):
    rows, width = tokens.shape
    row = pl.BlockSpec((block, width), lambda i: (i, 0))
    return call(
        functools.partial(tokens_back_kernel, len(dn_far)),
        (rows // block,),
        [row] * (3 + len(dn_far)) + [fixed(1, width)],
        row,
        shape((rows, width), F32),
        20 * rows * width,
        14 * rows * width,
    )(dn, *dn_far, tokens, grad, gain)


def project_back_kernel(dq_ref, dk_ref, dv_ref, wq_ref, wk_ref, wv_ref, tokens_ref, out_ref, sums_ref):
    total = mm(dq_ref[...], wq_ref[...], NT) + mm(dk_ref[...], wk_ref[...], NT) + mm(dv_ref[...], wv_ref[...], NT)
    out_ref[...] = total.astype(out_ref.dtype)
    normal, _ = normalise(tokens_ref[...].astype(F32))
    column_sums(sums_ref, total * normal, total)


def project_back(grads, weight, tokens, piece, dtype):
    rows = tokens.shape[0]
    width = grads[0].shape[1]
    depth = weight.shape[0]
    start = depth // width
    block = rows // 2
    part = pl.BlockSpec((block, width), lambda i: (2 * piece + i, 0))
    row = pl.BlockSpec((block, depth), lambda i: (i, 0))
    return call(
        project_back_kernel,
        (2,),
        [part] * 3 + [pl.BlockSpec((depth, width), lambda i, k=k: (0, start + k)) for k in range(3)] + [row],
        [row, fixed(8, depth)],
        [shape((rows, depth), dtype), shape((8, depth), F32)],
        6 * rows * width * depth,
        6 * depth * width + 6 * rows * width + 6 * rows * depth,
    )(*grads, weight, weight, weight, tokens)


def unpack_down(block, rows, width):
    parts = block.shape[1] // width
    if parts == 1:
        return block
    owners = block.shape[0] // rows
    return jnp.concatenate(
        [block[f * rows : (f + 1) * rows, j * width : (j + 1) * width] for f in range(owners) for j in range(parts)], axis=0
    )


def feed_kernel(owned, x_ref, og_ref, up_ref, down_ref, b_ref, act_ref, pre_ref, dn_ref, out_ref, sums_ref, dn_sum, out_sum):
    step, last = pl.program_id(0), pl.num_programs(0) - 1
    width = x_ref.shape[1]
    up = up_ref[...]
    down = unpack_down(down_ref[...], owned, width)
    u = mm(x_ref[...], up) + b_ref[...]
    phi = 0.5 * (1.0 + lax.erf(u * 0.7071067811865476))
    slope = phi + u * jnp.exp(-0.5 * u * u) * 0.3989422804014327
    act = (u * phi).astype(BF)
    act_ref[...] = act
    pre = (mm(og_ref[...], down, NT) * slope).astype(BF)
    pre_ref[...] = pre
    sums_ref[...] = jnp.sum(pre.astype(F32), axis=0, keepdims=True)
    dn = mm(pre, up, NT)
    out = mm(act, down)

    @pl.when(step == 0)
    def _():
        dn_sum[...] = dn
        out_sum[...] = out

    @pl.when(step > 0)
    def _():
        dn_sum[...] += dn
        out_sum[...] += out

    @pl.when(step == last)
    def _():
        dn_ref[...] = dn_sum[...].astype(dn_ref.dtype)
        out_ref[...] = out_sum[...].astype(out_ref.dtype)


def feed(x, og, up, down, bias, owned, dtype, block=512):
    rows, width = x.shape
    hidden = bias.shape[1]
    block = min(block, hidden)
    steps = hidden // block
    down_rows = down.shape[0] // steps
    down_columns = hidden if down.shape[1] > width else width
    columns = pl.BlockSpec((rows, block), lambda i: (0, i))
    vector = pl.BlockSpec((1, block), lambda i: (0, i))
    return call(
        functools.partial(feed_kernel, owned),
        (steps,),
        [
            fixed(rows, width),
            fixed(rows, width),
            pl.BlockSpec((width, block), lambda i: (0, i)),
            pl.BlockSpec((down_rows, down_columns), lambda i: (i, down.shape[1] // down_columns - 1)),
            vector,
        ],
        [columns, columns, fixed(rows, width), fixed(rows, width), vector],
        [
            shape((rows, hidden), BF),
            shape((rows, hidden), BF),
            shape((rows, width), dtype),
            shape((rows, width), dtype),
            shape((1, hidden), F32),
        ],
        8 * rows * width * hidden,
        4 * width * hidden + rows * (4 * hidden + 8 * width),
        2 * rows * hidden,
        [pltpu.VMEM((rows, width), F32)] * 2,
    )(x, og, up, down, bias)


def feed_grad_kernel(owned, count, *refs):
    xs, pres, acts, ogs = (refs[k * count : (k + 1) * count] for k in range(4))
    out_ref = refs[4 * count]
    ups = pl.num_programs(0) // 2
    step = pl.program_id(0)

    @pl.when(step < ups)
    def _():
        out_ref[...] = functools.reduce(jnp.add, [mm(x[...], p[...], TN) for x, p in zip(xs, pres)]).astype(BF)

    @pl.when(step >= ups)
    def _():
        grad = functools.reduce(jnp.add, [mm(a[...], g[...], TN) for a, g in zip(acts, ogs)]).astype(BF)
        width = grad.shape[1]
        parts = out_ref.shape[1] // width
        for f in range(out_ref.shape[0] // owned):
            for j in range(parts):
                start = (f * parts + j) * owned
                out_ref[f * owned : (f + 1) * owned, j * width : (j + 1) * width] = grad[start : start + owned, :]


def feed_grad(xs, pres, acts, ogs, owned, block=256):
    rows, width = xs[0].shape
    hidden = pres[0].shape[1]
    ups = width // block
    tall = block * hidden // width
    first = lambda i: (0, jnp.minimum(i, ups - 1))
    second = lambda i: (0, jnp.maximum(i - ups, 0))
    count = len(xs)
    return call(
        functools.partial(feed_grad_kernel, owned, count),
        (2 * ups,),
        [pl.BlockSpec((rows, block), first)] * count
        + [fixed(rows, hidden)] * count
        + [pl.BlockSpec((rows, tall), second)] * count
        + [fixed(rows, width)] * count,
        pl.BlockSpec((block, hidden), lambda i: (lax.rem(i, ups), lax.div(i, ups))),
        shape((width, 2 * hidden), BF),
        4 * count * rows * width * hidden,
        count * rows * (4 * width + 4 * hidden) + 4 * width * hidden,
    )(*xs, *pres, *acts, *ogs)


def attention_grad_kernel(att_ref, branch_ref, x_ref, dq_ref, dk_ref, dv_ref, small_ref, out_ref):
    width, n = branch_ref.shape[1], dq_ref.shape[1]
    out_ref[:, :width] = mm(att_ref[...], branch_ref[...], TN).astype(BF)
    x = x_ref[...]
    for k, ref in enumerate((dq_ref, dk_ref, dv_ref)):
        out_ref[:, width + k * n : width + (k + 1) * n] = mm(x, ref[...], TN).astype(BF)
    out_ref[:, width + 3 * n :] = small_ref[...].T.astype(BF)


def attention_grad(att, branch, x, grads, small, block=256):
    rows, depth = x.shape
    own = att.shape[0]
    width = grads[0].shape[1]
    columns = depth + 3 * width + SMALL
    return call(
        attention_grad_kernel,
        (depth // block,),
        [pl.BlockSpec((own, block), lambda i: (0, i)), fixed(own, depth), pl.BlockSpec((rows, block), lambda i: (0, i))]
        + [fixed(rows, width)] * 3
        + [pl.BlockSpec((SMALL, block), lambda i: (0, i))],
        pl.BlockSpec((block, columns), lambda i: (i, 0)),
        shape((depth, columns), BF),
        6 * rows * depth * width + 2 * own * depth * depth,
        2 * rows * (depth + 3 * width) + 2 * depth * columns,
    )(att, branch, x, *grads, small)


def after(values, *earlier):
    return lax.optimization_barrier((values, earlier))[0]


def on_device(
    tokens, positions, ln1_gain, ln1_bias, qkv_weight, qkv_bias, out_weight, out_bias,
    ln2_gain, ln2_bias, fc1_weight, fc1_bias, fc2_weight, fc2_bias, out_grad,
):
    rows, width = tokens.shape[1], tokens.shape[2]
    depth = qkv_weight.shape[0]
    owners, group = width // depth, lax.axis_size(SEQ)
    me, side = lax.axis_index(SHARD), lax.axis_index(SEQ)
    others = range(1, group)
    heads = width // group
    hidden_owned = fc2_weight.shape[0] // group
    packs = hidden_owned % depth == 0

    def gather(values):
        return lax.all_gather(values, SHARD, axis=0, tiled=True)

    def scatter(values):
        return lax.psum_scatter(values, SHARD, scatter_dimension=0, tiled=True)

    def spread(values):
        return [values] + [lax.ppermute(values, SEQ, shifted(group, d)) for d in others]

    def in_order(parts):
        stacked = jnp.stack(parts)
        return [take(stacked, (k - side) % group, 0) for k in range(group)]

    own_qkv = take(qkv_weight.reshape(depth, 3, group, heads), side, 2).reshape(depth, 3 * heads)
    names = (ln1_gain, ln1_bias, out_bias, ln2_gain, ln2_bias, fc2_bias, qkv_bias, fc1_bias)
    columns = [p.reshape(-1, depth).T for p in names]
    counts = [c.shape[1] for c in columns]
    extra = jnp.pad(jnp.concatenate(columns, axis=1), ((0, 0), (0, SMALL - sum(counts))))
    w_att = gather(jnp.concatenate([out_weight, own_qkv, extra], axis=1))
    own_up = take(fc1_weight.reshape(depth, owners, group, hidden_owned), side, 2).reshape(depth, -1)
    own_down = take(fc2_weight.reshape(group, hidden_owned, width), side, 0)
    if packs:
        own_down = own_down.reshape(-1, depth, width).transpose(1, 0, 2).reshape(depth, -1)
        w_up = w_down = gather(jnp.concatenate([own_up, own_down], axis=1))
    else:
        w_up, w_down = gather(own_up), gather(own_down)

    clip = spread(tokens[0])
    places = jnp.concatenate(spread(positions[:, 0, :].astype(F32)), axis=1)
    grads = spread(out_grad[0])

    tables = rotary_tables(places)
    normal_one, _ = normalise(jnp.concatenate(clip, axis=0).astype(F32))

    start = width + 3 * heads
    lines = w_att[:, start : start + SMALL].astype(F32).T[: sum(counts)]
    vectors, at = [], 0
    for n in counts:
        vectors.append(lines[at : at + n].reshape(n, owners, depth).transpose(1, 0, 2).reshape(1, -1))
        at += n
    gain_one, bias_one, b_out, gain_two, bias_two, b_down, b_qkv, b_up = vectors
    b_qkv = take(b_qkv.reshape(3, group, heads), side, 1).reshape(1, -1)
    b_up = take(b_up.reshape(owners, group, hidden_owned), side, 1).reshape(1, -1)

    normed_one = after((normal_one * gain_one + bias_one).astype(BF), grads)
    qkv = project(normed_one, w_att, b_qkv, tables, heads)
    att, lse = attend(qkv)

    mine = [att[:rows]] + [lax.ppermute(att[d * rows : (d + 1) * rows], SEQ, shifted(group, -d)) for d in others]
    att_rows = jnp.concatenate(in_order(mine), axis=1)
    hidden, normed_two = project_out(att_rows, w_att, tokens[0], b_out, gain_two, bias_two)
    normed = spread(normed_two)

    fed = [feed(x, g, w_up, w_down, b_up, depth, F32 if d == 0 else BF) for d, (x, g) in enumerate(zip(normed, grads))]
    acts, pres, dns, outs, sums = zip(*fed)
    dn_far = [lax.ppermute(dns[d], SEQ, shifted(group, -d)) for d in others]
    out_far = [lax.ppermute(outs[d], SEQ, shifted(group, -d)) for d in others]

    if packs:
        fed_grads = feed_grad(normed, pres, acts, grads, depth)
        fed_sum = scatter(fed_grads)
        dns = (after(dns[0], fed_grads),) + dns[1:]
    hidden_grad, branch, att_grad, sums_two = hidden_back(dns[0], dn_far, hidden, out_grad[0], gain_two, w_att)
    shares = att_grad.reshape(rows, group, heads)
    att_grads = [take(shares, side, 1)]
    att_grads += [lax.ppermute(take(shares, (side + d) % group, 1), SEQ, shifted(group, d)) for d in others]

    qkv_grads = attend_back(qkv, att, lse, jnp.concatenate(att_grads, axis=0), tables)
    parts_one = [project_back(qkv_grads, w_att, clip[d], d, F32 if d == 0 else BF) for d in range(group)]
    dn_one, sums_one = zip(*parts_one)
    dn_one_far = [lax.ppermute(dn_one[d], SEQ, shifted(group, -d)) for d in others]

    here = (jnp.arange(group) == side).astype(F32)
    qkv_b = jnp.stack([jnp.sum(g.astype(F32), axis=0) for g in qkv_grads])[:, None, :] * here[None, :, None]
    up_b = functools.reduce(jnp.add, sums).reshape(owners, 1, hidden_owned) * here[None, :, None]
    sums_one = functools.reduce(jnp.add, sums_one)
    vectors = (sums_one[0], sums_one[1], sums_two[2], sums_two[0], sums_two[1], sums_two[3], qkv_b, up_b)
    lines = [v.reshape(owners, n, depth).transpose(1, 0, 2).reshape(n, width) for v, n in zip(vectors, counts)]
    lines = jnp.pad(jnp.concatenate(lines, axis=0), ((0, SMALL - sum(counts)), (0, 0)))
    att_grads = attention_grad(att_rows, branch, normed_one, qkv_grads, lines)
    att_sum = scatter(after(att_grads, fed_sum) if packs else att_grads)
    tokens_grad = tokens_back(dn_one[0], dn_one_far, tokens[0], hidden_grad, gain_one)

    block_out = hidden + outs[0] + b_down
    for far in out_far:
        block_out = block_out + far.astype(F32)

    if packs:
        up_sum, down_sum = fed_sum[:, : own_up.shape[1]], fed_sum[:, own_up.shape[1] :]
        down_sum = down_sum.reshape(depth, -1, width).transpose(1, 0, 2).reshape(-1, width)
    else:
        up_sum = scatter(functools.reduce(jnp.add, [mm(x, p, TN) for x, p in zip(normed, pres)]).astype(BF))
        down_sum = scatter(functools.reduce(jnp.add, [mm(a, g, TN) for a, g in zip(acts, grads)]).astype(BF))

    def joined(values):
        return in_order([values] + [lax.ppermute(values, SEQ, shifted(group, -d)) for d in others])

    att_all = joined(att_sum)
    once = functools.reduce(jnp.add, [v.astype(F32) for v in att_all])
    out_total, columns = once[:, :width], once[:, width + 3 * heads :]
    qkv_total = jnp.stack([v[:, width : width + 3 * heads].reshape(depth, 3, heads) for v in att_all], axis=2)
    qkv_total = qkv_total.reshape(depth, -1).astype(F32)
    up_total = jnp.stack([v.reshape(depth, owners, hidden_owned) for v in joined(up_sum)], axis=2).reshape(depth, -1).astype(F32)
    down_total = jnp.concatenate(joined(down_sum), axis=0).astype(F32)

    lines, ends = columns.T, np.cumsum(counts)
    g1, b1, bo, g2, b2, bd, bq, bu = [lines[e - n : e].reshape(-1) for e, n in zip(ends, counts)]
    return (
        block_out.astype(BF)[None], tokens_grad[None], g1, b1, qkv_total, bq, out_total, bo, g2, b2, up_total, bu,
        down_total, bd,
    )


def solution(mesh):
    vector, matrix, tokens = P(SHARD), P(SHARD, None), P(SHARD, SEQ, None)
    return jax.shard_map(
        on_device,
        mesh=mesh,
        in_specs=(
            tokens, P(None, SHARD, SEQ), vector, vector, matrix, vector, matrix, vector, vector, vector, matrix, vector,
            matrix, vector, tokens,
        ),
        out_specs=(
            tokens, tokens, vector, vector, matrix, vector, matrix, vector, vector, vector, matrix, vector, matrix, vector
        ),
        check_vma=False,
    )
```

```python
import functools

import jax
import jax.numpy as jnp
import numpy as np
from jax import lax
from jax.experimental import pallas as pl
from jax.experimental.pallas import tpu as pltpu
from jax.sharding import Mesh, PartitionSpec as P

HD = 64
EPS = 1e-06
THETA = 10000.0
LOG2E = 1.4426950408889634
SCALE = HD**-0.5
BF = jnp.bfloat16
F32 = jnp.float32
NT = (((1,), (1,)), ((), ()))
TN = (((0,), (0,)), ((), ()))
NN = (((1,), (0,)), ((), ()))
SMALL = 128
VMEM_BYTES = 56 << 20
LOW, HIGH = 0.25, 200
SHARD = ("o", "i", "c")
SEQ = "seq"


def mm(a, b, dims=NN):
    return lax.dot_general(a, b, dims, preferred_element_type=F32)


def shifted(size, by):
    return [(i, (i + by) % size) for i in range(size)]


def take(values, index, axis):
    return lax.dynamic_index_in_dim(values, index, axis, keepdims=False)


def shape(dims, dtype):
    return jax.ShapeDtypeStruct(dims, dtype)


def fixed(*dims):
    return pl.BlockSpec(dims, lambda *_: (0,) * len(dims))


def spec(block, index):
    return pl.BlockSpec(block, index)


def call(kernel, grid, in_specs, out_specs, out_shape, flops, moved, exps=0, scratch=(), scalars=0, weight=LOW):
    return pl.pallas_call(
        kernel,
        grid_spec=pltpu.PrefetchScalarGridSpec(
            num_scalar_prefetch=scalars,
            grid=grid,
            in_specs=in_specs,
            out_specs=out_specs,
            scratch_shapes=list(scratch),
        ),
        out_shape=out_shape,
        compiler_params=pltpu.CompilerParams(vmem_limit_bytes=VMEM_BYTES),
        cost_estimate=pl.CostEstimate(flops=int(weight * flops), bytes_accessed=int(weight * moved), transcendentals=int(weight * exps)),
    )


def pick(parts, index):
    chosen = parts[0]
    for k in range(1, len(parts)):
        chosen = jnp.where(index == k, parts[k], chosen)
    return chosen


def chips_in_line(mesh):
    chips = mesh.devices.shape[0] // 2
    places = [getattr(d, "coords", None) for d in mesh.devices[::2, 0]]
    if places[0] is None or chips < 2:
        return 2 if chips % 2 == 0 else 1
    axis = [a for a in range(3) if places[0][a] != places[1][a]][0]
    inner = 1
    while inner < chips and all(places[inner][a] == places[0][a] for a in range(3) if a != axis):
        inner += 1
    return inner


class Lines:
    def __init__(self, mesh):
        fsdp, seq = mesh.devices.shape
        self.chips = fsdp // 2
        self.inner = chips_in_line(mesh)
        self.outer = self.chips // self.inner
        self.mesh = Mesh(mesh.devices.reshape(self.outer, self.inner, 2, seq), SHARD + (SEQ,))
        self.outer_long = self.outer >= self.inner
        self.long, self.short = ("o", "i") if self.outer_long else ("i", "o")
        self.n_long, self.n_short = max(self.outer, self.inner), min(self.outer, self.inner)

    def place(self, long, short):
        return (long, short) if self.outer_long else (short, long)

    def split(self, values):
        return values.reshape(self.outer, self.inner, *values.shape[1:])

    def here(self):
        return jnp.stack([lax.axis_index(a) for a in (self.long, self.short, "c", SEQ)]).astype(jnp.int32)


def stack_kernel(lines, here, *refs):
    *pieces, out, sems = refs
    copies = []
    for n, piece in enumerate(pieces):
        back_short, back_long = n // lines.n_long, n % lines.n_long
        long = lax.rem(here[0] + (lines.n_long - back_long), lines.n_long)
        short = lax.rem(here[1] + (lines.n_short - back_short), lines.n_short)
        a, b = lines.place(long, short)
        copies.append(pltpu.make_async_copy(piece, out.at[a, b], sems.at[n]))
    for copy in copies:
        copy.start()
    for copy in copies:
        copy.wait()


def staged_gather(lines, here, values, meanwhile):
    line = [values] + [lax.ppermute(values, lines.long, shifted(lines.n_long, d)) for d in range(1, lines.n_long)]
    pieces = list(line)
    for d in range(1, lines.n_short):
        pieces += [lax.ppermute(v, lines.short, shifted(lines.n_short, d)) for v in line]
    dims = (lines.outer, lines.inner) + values.shape
    pieces = after(pieces, meanwhile)
    mine = call(
        functools.partial(stack_kernel, lines),
        (1,),
        [pl.BlockSpec(memory_space=pl.ANY)] * len(pieces),
        pl.BlockSpec(dims, lambda *_: (0,) * 4),
        shape(dims, values.dtype),
        0,
        4 * lines.chips * values.size,
        scratch=[pltpu.SemaphoreType.DMA((len(pieces),))],
        scalars=1,
    )(here, *pieces)
    mine = mine.reshape((lines.chips,) + values.shape)
    return mine, lax.ppermute(mine, "c", shifted(2, 1))


def add_first_kernel(here, keep_ref, got_ref, out_ref):
    out_ref[...] = (keep_ref[...].astype(F32) + got_ref[...].astype(F32)).astype(BF)


def add_second_kernel(lines, late, here, keep_ref, got_ref, *refs):
    ins, refs = refs[: lines.n_short - 1], refs[lines.n_short - 1 :]
    late_ref, outs = (refs[0], refs[1:]) if late else (None, refs)
    for k, out in enumerate(outs):
        at = lines.place(lax.rem(here[0] + k, lines.n_long), 0)
        total = keep_ref[at].astype(F32) + got_ref[at].astype(F32)
        for r in ins:
            total = total + r[at].astype(F32)
        if late:
            n = total.shape[1] - SMALL
            out[:, :n] = total[:, :n].astype(BF)
            out[:, n:] = (total[:, n:] + late_ref[at[0] + at[1]]).astype(BF)
        else:
            out[...] = total.astype(BF)


def add_last_kernel(*refs):
    *ins, out = refs
    out[...] = functools.reduce(jnp.add, [r[...].astype(F32) for r in ins]).astype(BF)


class StagedSum:
    def __init__(self, lines, here, keep, send):
        self.lines, self.here = lines, here
        self.got = lines.split(lax.ppermute(send, "c", shifted(2, 1)))
        self.keep = lines.split(keep)
        self.rows, self.columns = keep.shape[1:]
        self.dims = lines.place(lines.n_long, 1) + (self.rows, self.columns)
        self.size = lines.n_long * self.rows * self.columns

    def across(self, d):
        lines = self.lines
        return pl.BlockSpec(self.dims, lambda i, h: lines.place(0, lax.rem(h[1] + d, lines.n_short)) + (0, 0))

    def short(self):
        lines, dims = self.lines, self.dims
        away = [
            call(
                add_first_kernel,
                (1,),
                [self.across(d)] * 2,
                pl.BlockSpec(dims, lambda i, h: (0, 0, 0, 0)),
                shape(dims, BF),
                self.size,
                6 * self.size,
                scalars=1,
            )(self.here, self.keep, self.got)
            for d in range(1, lines.n_short)
        ]
        self.arrived = [lax.ppermute(v, lines.short, shifted(lines.n_short, d + 1)) for d, v in enumerate(away)]
        return away

    def long(self, late=()):
        lines = self.lines
        flat = pl.BlockSpec((self.rows, self.columns), lambda i, h: (0, 0))
        parts = call(
            functools.partial(add_second_kernel, lines, len(late) > 0),
            (1,),
            [self.across(0)] * 2
            + [pl.BlockSpec(self.dims, lambda i, h: (0, 0, 0, 0))] * len(self.arrived)
            + [fixed(*v.shape) for v in late],
            [flat] * lines.n_long,
            [shape((self.rows, self.columns), BF)] * lines.n_long,
            3 * self.size,
            8 * self.size,
            scalars=1,
        )(self.here, self.keep, self.got, *self.arrived, *late)
        self.parts = [parts[0]]
        self.parts += [lax.ppermute(parts[d], lines.long, shifted(lines.n_long, d)) for d in range(1, lines.n_long)]
        return parts

    def last(self):
        return call(
            add_last_kernel,
            (1,),
            [fixed(self.rows, self.columns)] * len(self.parts),
            fixed(self.rows, self.columns),
            shape((self.rows, self.columns), BF),
            self.size,
            3 * self.size,
        )(*self.parts)


def share_kernel(group, here, qkv_ref, up_ref, down_ref, out_ref, *refs):
    *small_refs, att_ref, feed_ref = refs
    side = here[3]
    depth, width = out_ref.shape
    heads = width // group
    for k in range(3):
        parts = [qkv_ref[:, k * width + g * heads : k * width + (g + 1) * heads] for g in range(group)]
        att_ref[:, k * heads : (k + 1) * heads] = pick(parts, side)
    rows = [r[:, j : j + depth].astype(F32) for r in small_refs for j in range(0, r.shape[1], depth)]
    rows.append(jnp.zeros((SMALL - len(rows), depth), F32))
    att_ref[:, 3 * heads :] = jnp.concatenate(rows, axis=0).T.astype(BF)
    owned = down_ref.shape[0] // group
    hidden = up_ref.shape[1] // group
    for f in range(hidden // owned):
        parts = [up_ref[:, (f * group + g) * owned : (f * group + g + 1) * owned] for g in range(group)]
        feed_ref[:, f * owned : (f + 1) * owned] = pick(parts, side)
    for j in range(owned // depth):
        parts = [down_ref[g * owned + j * depth : g * owned + (j + 1) * depth, :] for g in range(group)]
        feed_ref[:, hidden + j * width : hidden + (j + 1) * width] = pick(parts, side)
    feed_ref[:, 2 * hidden :] = out_ref[...]


def share(here, group, qkv, up, down, out, small):
    depth, width = out.shape
    args = (qkv, up, down, out, *[v.reshape(1, -1) for v in small])
    att, feed_columns = qkv.shape[1] // group + SMALL, 2 * up.shape[1] // group + width
    return call(
        functools.partial(share_kernel, group),
        (1,),
        [fixed(*a.shape) for a in args],
        [fixed(depth, att), fixed(depth, feed_columns)],
        [shape((depth, att), BF), shape((depth, feed_columns), BF)],
        0,
        8 * depth * (att + feed_columns),
        scalars=1,
    )(here, *args)


def finish_attention_kernel(group, here, *refs):
    shares, (out_ref, qkv_ref, small_ref) = refs[:group], refs[group:]
    width = out_ref.shape[1]
    heads = width // group
    total = functools.reduce(jnp.add, [r[:, :width].astype(F32) for r in shares])
    out_ref[...] = total
    small = functools.reduce(jnp.add, [r[:, -SMALL:].astype(F32) for r in shares])
    small_ref[...] = small.T
    for k in range(group):
        source = lax.rem(k - here[3] + group, group)
        for m in range(3):
            at, start = m * width + k * heads, width + m * heads
            parts = [r[:, start : start + heads] for r in shares]
            qkv_ref[:, at : at + heads] = pick(parts, source).astype(F32)


def finish_attention(here, shares, width):
    depth, group = shares[0].shape[0], len(shares)
    return call(
        functools.partial(finish_attention_kernel, group),
        (1,),
        [fixed(*v.shape) for v in shares],
        [fixed(depth, width), fixed(depth, 3 * width), fixed(SMALL, depth)],
        [shape((depth, width), F32), shape((depth, 3 * width), F32), shape((SMALL, depth), F32)],
        0,
        24 * depth * width,
        scalars=1,
    )(here, *shares)


def finish_feed_kernel(group, here, *refs):
    shares, (up_ref, down_ref) = refs[:group], refs[group:]
    depth, width = shares[0].shape[0], down_ref.shape[1]
    owned = down_ref.shape[0] // group
    hidden = up_ref.shape[1] // group
    for k in range(group):
        source = lax.rem(k - here[3] + group, group)
        for f in range(hidden // owned):
            at = (f * group + k) * owned
            up_ref[:, at : at + owned] = pick([r[:, f * owned : (f + 1) * owned] for r in shares], source).astype(F32)
        for j in range(owned // depth):
            at, start = k * owned + j * depth, hidden + j * width
            down_ref[at : at + depth, :] = pick([r[:, start : start + width] for r in shares], source).astype(F32)


def finish_feed(here, shares, up_shape, down_shape):
    return call(
        functools.partial(finish_feed_kernel, len(shares)),
        (1,),
        [fixed(*v.shape) for v in shares],
        [fixed(*up_shape), fixed(*down_shape)],
        [shape(up_shape, F32), shape(down_shape, F32)],
        0,
        12 * up_shape[0] * up_shape[1],
        scalars=1,
    )(here, *shares)


def rotated(values, cos, low, high):
    half = 2 * (HD // 3 // 2) // 2
    return values * cos + pltpu.roll(values, values.shape[1] - half, 1) * low + pltpu.roll(values, half, 1) * high


def project_kernel(here, x_ref, mine_ref, sib_ref, b_ref, cos_ref, low_ref, high_ref, out_ref, w_ref):
    rows = mine_ref.shape[1]
    core = here[2]
    for q in range(mine_ref.shape[0]):
        w_ref[pl.ds(pl.multiple_of((2 * q + core) * rows, rows), rows), :] = mine_ref[q]
        w_ref[pl.ds(pl.multiple_of((2 * q + 1 - core) * rows, rows), rows), :] = sib_ref[q]
    values = mm(x_ref[...], w_ref[...]) + b_ref[...]
    width = values.shape[1]

    @pl.when(pl.program_id(0) < 2)
    def _():
        cos, low, high = cos_ref[...], low_ref[...], high_ref[...]
        for j in range(0, width, 128):
            out_ref[:, j : j + 128] = rotated(values[:, j : j + 128], cos, low, high).astype(BF)

    @pl.when(pl.program_id(0) >= 2)
    def _():
        out_ref[...] = values.astype(BF)


def project(here, x, mine, sib, bias, tables, width):
    rows, depth = x.shape
    part = pl.BlockSpec(mine.shape[:2] + (width,), lambda i, h: (0, 0, i))
    return call(
        project_kernel,
        (3,),
        [fixed(rows, depth), part, part, pl.BlockSpec((1, width), lambda i, h: (0, i))] + [fixed(rows, 128)] * 3,
        [pl.BlockSpec((rows, width), lambda i, h: (0, i)), pl.BlockSpec((depth, width), lambda i, h: (0, i))],
        [shape((rows, 3 * width), BF), shape((depth, 3 * width), BF)],
        6 * rows * depth * width,
        12 * depth * width + 2 * rows * (depth + 3 * width),
        scalars=1,
    )(here, x, mine, sib, bias, *tables)


def rotary_tables(positions):
    width = 2 * (HD // 3 // 2)
    half = width // 2
    freqs = np.power(np.float32(THETA), -(np.arange(half, dtype=np.float32) * np.float32(2.0 / width)))
    column = np.arange(2 * HD) % HD
    turns = column < 3 * width
    axis = np.minimum(column // width, 2)
    freq = np.where(turns, freqs[column % half], 0.0).astype(np.float32)
    leading = turns & (column % width < half)
    trailing = turns & (column % width >= half)
    place = jnp.where(axis == 0, positions[0][:, None], jnp.where(axis == 1, positions[1][:, None], positions[2][:, None]))
    angle = place * freq
    sine = jnp.sin(angle)
    return jnp.cos(angle), jnp.where(leading, -sine, 0.0), jnp.where(trailing, sine, 0.0)


def over_blocks(rows, block, step):
    if rows // block <= 4:
        for i in range(rows // block):
            step(pl.ds(i * block, block))
    else:

        def body(i, carry):
            step(pl.ds(pl.multiple_of(i * block, block), block))
            return carry

        lax.fori_loop(0, rows // block, body, 0)


def attend_kernel(block, q_ref, k_ref, v_ref, o_ref, lse_ref):
    rows = q_ref.shape[0]
    first = lax.broadcasted_iota(jnp.int32, (1, 128), 1) < HD
    factor = jnp.float32(SCALE * LOG2E)
    zero = jnp.zeros((), BF)

    def step(rs):
        q = q_ref[rs, :]
        outs, lses = [], []
        for h in range(2):
            mine = first if h == 0 else jnp.logical_not(first)
            scores = mm(jnp.where(mine, q, zero), k_ref[...], NT)
            peak = jnp.max(scores, axis=1, keepdims=True) * factor
            weights = jnp.exp2(scores * factor - peak)
            total = jnp.sum(weights, axis=1, keepdims=True)
            outs.append(mm(weights.astype(BF), v_ref[...]) * (1.0 / total))
            lses.append(peak + jnp.log2(total))
        o_ref[rs, :] = jnp.where(first, outs[0], outs[1]).astype(BF)
        lse_ref[rs, :] = jnp.where(first, lses[0], lses[1])

    over_blocks(rows, block, step)


def attend_back_kernel(
    block, q_ref, k_ref, v_ref, o_ref, lse_ref, do_ref, cos_ref, low_ref, high_ref, dq_ref, dk_ref, dv_ref, sums_ref, dk_sum, dv_sum
):
    rows = q_ref.shape[0]
    first = lax.broadcasted_iota(jnp.int32, (1, 128), 1) < HD
    factor = jnp.float32(SCALE * LOG2E)
    zero = jnp.zeros((), BF)
    dk_sum[...] = jnp.zeros_like(dk_sum)
    dv_sum[...] = jnp.zeros_like(dv_sum)

    def step(rs):
        q, do = q_ref[rs, :], do_ref[rs, :]
        od = o_ref[rs, :].astype(F32) * do.astype(F32)
        lse = lse_ref[rs, :]
        dq = None
        for h in range(2):
            mine = first if h == 0 else jnp.logical_not(first)
            qh, doh = jnp.where(mine, q, zero), jnp.where(mine, do, zero)
            delta = jnp.sum(jnp.where(mine, od, 0.0), axis=1, keepdims=True)
            k = k_ref[...]
            p = jnp.exp2(mm(qh, k, NT) * factor - lse[:, h * HD : h * HD + 1])
            ds = (p * (mm(doh, v_ref[...], NT) - delta)).astype(BF)
            dv_sum[...] += mm(p.astype(BF), doh, TN)
            dk_sum[...] += mm(ds, qh, TN)
            part = mm(ds, jnp.where(mine, k, zero))
            dq = part if dq is None else dq + part
        dq = (dq * SCALE).astype(BF).astype(F32)
        dq_ref[rs, :] = rotated(dq, cos_ref[rs, :], -low_ref[rs, :], -high_ref[rs, :]).astype(BF)

    over_blocks(rows, block, step)
    dk = (dk_sum[...] * SCALE).astype(BF).astype(F32)
    dk_ref[...] = rotated(dk, cos_ref[...], -low_ref[...], -high_ref[...]).astype(BF)
    dv_ref[...] = dv_sum[...].astype(BF)
    sums = [jnp.sum(r[...].astype(F32), axis=0, keepdims=True) for r in (dq_ref, dk_ref, dv_ref)]
    sums_ref[...] = jnp.concatenate(sums + [jnp.zeros((5, 128), F32)], axis=0)


def pair_spec(rows, first=0):
    return pl.BlockSpec((rows, 128), lambda i: (0, first + i))


def attend(qkv, block=512):
    rows, columns = qkv.shape[0], qkv.shape[1] // 3
    pairs = columns // 128
    return call(
        functools.partial(attend_kernel, min(block, (1 << 19) // rows)),
        (pairs,),
        [pair_spec(rows, k * pairs) for k in range(3)],
        [pair_spec(rows)] * 2,
        [shape((rows, columns), BF), shape((rows, columns), F32)],
        16 * rows * rows * columns,
        rows * columns * 12,
        rows * rows * columns // HD,
    )(qkv, qkv, qkv)


def attend_back(qkv, o, lse, do, tables, block=512):
    rows, columns = o.shape
    pairs = columns // 128
    return call(
        functools.partial(attend_back_kernel, min(block, (1 << 19) // rows)),
        (pairs,),
        [pair_spec(rows, k * pairs) for k in range(3)] + [pair_spec(rows)] * 3 + [fixed(rows, 128)] * 3,
        [pair_spec(rows)] * 3 + [pl.BlockSpec((8, 128), lambda i: (0, i))],
        [shape((rows, columns), BF)] * 3 + [shape((8, columns), F32)],
        40 * rows * rows * columns,
        rows * columns * 20,
        rows * rows * columns // HD,
        [pltpu.VMEM((rows, 128), F32)] * 2,
    )(qkv, qkv, qkv, o, lse, do, *tables)


def normalise(values):
    center = values - jnp.mean(values, axis=-1, keepdims=True)
    factor = lax.rsqrt(jnp.mean(center * center, axis=-1, keepdims=True) + EPS)
    return center * factor, factor


def normalise_back(grads, gain, normal, factor):
    e = grads * gain
    inner = e - jnp.mean(e, axis=-1, keepdims=True) - normal * jnp.mean(e * normal, axis=-1, keepdims=True)
    return factor * inner


def column_sums(out_ref, *parts):
    sums = [jnp.sum(p, axis=0, keepdims=True) for p in parts]
    sums.append(jnp.zeros((8 - len(sums), sums[0].shape[1]), F32))
    block = jnp.concatenate(sums, axis=0)

    @pl.when(pl.program_id(0) == 0)
    def _():
        out_ref[...] = block

    @pl.when(pl.program_id(0) > 0)
    def _():
        out_ref[...] += block


def out_kernel(group, here, *refs):
    atts, weights, (tokens_ref, b_ref, gain_ref, bias_ref, hidden_ref, normed_ref) = (
        refs[:group],
        refs[group : 2 * group],
        refs[2 * group :],
    )
    hidden = tokens_ref[...].astype(F32) + b_ref[...]
    for att, w in zip(atts, weights):
        hidden = hidden + mm(att[...], w[...])
    hidden_ref[...] = hidden
    normed_ref[...] = (normalise(hidden)[0] * gain_ref[...] + bias_ref[...]).astype(BF)


def project_out(here, atts, weight, at, tokens, b, gain, bias, block=256):
    rows, width = tokens.shape
    group, heads = len(atts), atts[0].shape[1]
    row = pl.BlockSpec((block, width), lambda i, h: (i, 0))
    return call(
        functools.partial(out_kernel, group),
        (rows // block,),
        [pl.BlockSpec((block, heads), lambda i, h: (i, 0))] * group
        + [pl.BlockSpec((heads, width), lambda i, h, d=d: (lax.rem(h[3] + d, group), at)) for d in range(group)]
        + [row]
        + [fixed(1, width)] * 3,
        [row, row],
        [shape((rows, width), F32), shape((rows, width), BF)],
        2 * rows * width * width,
        2 * width * width + 10 * rows * width,
        scalars=1,
    )(here, *atts, *[weight] * group, tokens, b, gain, bias)


def hidden_back_kernel(group, here, *refs):
    dn_ref, far_refs, (hidden_ref, og_ref, gain_ref, w_ref, grad_ref, branch_ref, sums_ref, *att_refs) = (
        refs[0],
        refs[1:group],
        refs[group:],
    )
    dn = dn_ref[...]
    for far in far_refs:
        dn = dn + far[...].astype(F32)
    normal, factor = normalise(hidden_ref[...])
    og = og_ref[...].astype(F32)
    grad = og + normalise_back(dn, gain_ref[...], normal, factor)
    grad_ref[...] = grad
    branch = grad.astype(BF)
    branch_ref[...] = branch
    att = mm(branch, w_ref[...], NT).astype(BF)
    heads = att.shape[1] // group
    parts = [att[:, k * heads : (k + 1) * heads] for k in range(group)]
    for d, ref in enumerate(att_refs):
        ref[...] = pick(parts, lax.rem(here[3] + d, group))
    column_sums(sums_ref, dn * normal, dn, branch.astype(F32), og)


def hidden_back(here, dn, dn_far, hidden, og, gain, weight, at, block=256):
    rows, width = hidden.shape
    group = 1 + len(dn_far)
    row = pl.BlockSpec((block, width), lambda i, h: (i, 0))
    share = pl.BlockSpec((block, width // group), lambda i, h: (i, 0))
    return call(
        functools.partial(hidden_back_kernel, group),
        (rows // block,),
        [row] * group + [row, row, fixed(1, width), pl.BlockSpec((width, width), lambda i, h: (0, at))],
        [row, row, fixed(8, width)] + [share] * group,
        [shape((rows, width), F32), shape((rows, width), BF), shape((8, width), F32)]
        + [shape((rows, width // group), BF)] * group,
        2 * rows * width * width,
        2 * width * width + 18 * rows * width,
        scalars=1,
        weight=HIGH,
    )(here, dn, *dn_far, hidden, og, gain, weight)


def tokens_back_kernel(extra, *refs):
    dn_ref, far_refs, (tokens_ref, grad_ref, gain_ref, out_ref) = refs[0], refs[1 : 1 + extra], refs[1 + extra :]
    dn = dn_ref[...]
    for far in far_refs:
        dn = dn + far[...].astype(F32)
    normal, factor = normalise(tokens_ref[...].astype(F32))
    out_ref[...] = grad_ref[...] + normalise_back(dn, gain_ref[...], normal, factor)


def tokens_back(dn, dn_far, tokens, grad, gain, block=256):
    rows, width = tokens.shape
    row = pl.BlockSpec((block, width), lambda i: (i, 0))
    return call(
        functools.partial(tokens_back_kernel, len(dn_far)),
        (rows // block,),
        [row] * (3 + len(dn_far)) + [fixed(1, width)],
        row,
        shape((rows, width), F32),
        20 * rows * width,
        14 * rows * width,
    )(dn, *dn_far, tokens, grad, gain)


def project_back_kernel(dq_ref, dk_ref, dv_ref, w_ref, tokens_ref, out_ref, sums_ref):
    width = dq_ref.shape[1]
    total = functools.reduce(
        jnp.add,
        [mm(g[...], w_ref[:, k * width : (k + 1) * width], NT) for k, g in enumerate((dq_ref, dk_ref, dv_ref))],
    )
    out_ref[...] = total.astype(out_ref.dtype)
    normal, _ = normalise(tokens_ref[...].astype(F32))
    column_sums(sums_ref, total * normal, total)


def project_back(grads, weight, tokens, piece, rows, dtype):
    width, depth = grads[0].shape[1], tokens.shape[1]
    block = rows // 2
    row = pl.BlockSpec((block, depth), lambda i: (i, 0))
    return call(
        project_back_kernel,
        (2,),
        [pl.BlockSpec((block, width), lambda i: (2 * piece + i, 0))] * 3 + [fixed(depth, 3 * width), row],
        [row, fixed(8, depth)],
        [shape((rows, depth), dtype), shape((8, depth), F32)],
        6 * rows * width * depth,
        6 * width * depth + rows * (6 * width + 6 * depth),
    )(*grads, weight, tokens)


def unpack_down(block, rows, width):
    parts = block.shape[1] // width
    if parts == 1:
        return block
    owners = block.shape[0] // rows
    return jnp.concatenate(
        [block[f * rows : (f + 1) * rows, j * width : (j + 1) * width] for f in range(owners) for j in range(parts)], axis=0
    )


def feed_kernel(owned, x_ref, og_ref, up_ref, down_ref, b_ref, act_ref, pre_ref, dn_ref, out_ref, sums_ref, dn_sum, out_sum):
    step, last = pl.program_id(0), pl.num_programs(0) - 1
    width = x_ref.shape[1]
    up = up_ref[...]
    down = unpack_down(down_ref[...], owned, width)
    u = mm(x_ref[...], up) + b_ref[...]
    phi = 0.5 * (1.0 + lax.erf(u * 0.7071067811865476))
    slope = phi + u * jnp.exp(-0.5 * u * u) * 0.3989422804014327
    act = (u * phi).astype(BF)
    act_ref[...] = act
    pre = (mm(og_ref[...], down, NT) * slope).astype(BF)
    pre_ref[...] = pre
    sums_ref[...] = jnp.sum(pre.astype(F32), axis=0, keepdims=True)
    dn = mm(pre, up, NT)
    out = mm(act, down)

    @pl.when(step == 0)
    def _():
        dn_sum[...] = dn
        out_sum[...] = out

    @pl.when(step > 0)
    def _():
        dn_sum[...] += dn
        out_sum[...] += out

    @pl.when(step == last)
    def _():
        dn_ref[...] = dn_sum[...].astype(dn_ref.dtype)
        out_ref[...] = out_sum[...].astype(out_ref.dtype)


def feed(x, og, up, down, packs, bias, owned, dtype, block=512):
    rows, width = x.shape
    hidden = bias.shape[1]
    block = min(block, hidden)
    steps = hidden // block
    down_rows = down.shape[0] // steps
    down_columns = hidden if packs else width
    columns = pl.BlockSpec((rows, block), lambda i: (0, i))
    vector = pl.BlockSpec((1, block), lambda i: (0, i))
    return call(
        functools.partial(feed_kernel, owned),
        (steps,),
        [
            fixed(rows, width),
            fixed(rows, width),
            pl.BlockSpec((width, block), lambda i: (0, i)),
            pl.BlockSpec((down_rows, down_columns), lambda i: (i, int(packs))),
            vector,
        ],
        [columns, columns, fixed(rows, width), fixed(rows, width), vector],
        [
            shape((rows, hidden), BF),
            shape((rows, hidden), BF),
            shape((rows, width), dtype),
            shape((rows, width), dtype),
            shape((1, hidden), F32),
        ],
        8 * rows * width * hidden,
        4 * width * hidden + rows * (4 * hidden + 8 * width),
        2 * rows * hidden,
        [pltpu.VMEM((rows, width), F32)] * 2,
    )(x, og, up, down, bias)


def up_grad_kernel(count, *refs):
    xs, pres, (_, out_ref) = refs[:count], refs[count : 2 * count], refs[2 * count :]
    out_ref[...] = functools.reduce(jnp.add, [mm(x[...], p[...], TN) for x, p in zip(xs, pres)]).astype(BF)


def down_grad_kernel(owned, count, *refs):
    acts, ogs, out_ref = refs[:count], refs[count : 2 * count], refs[2 * count]
    grad = functools.reduce(jnp.add, [mm(a[...], g[...], TN) for a, g in zip(acts, ogs)]).astype(BF)
    width = grad.shape[1]
    parts = out_ref.shape[1] // width
    for f in range(out_ref.shape[0] // owned):
        for j in range(parts):
            start = (f * parts + j) * owned
            out_ref[f * owned : (f + 1) * owned, j * width : (j + 1) * width] = grad[start : start + owned, :]


def down_grad(acts, ogs, owned, block=256):
    count, (rows, hidden), width = len(acts), acts[0].shape, ogs[0].shape[1]
    steps = width // block
    return call(
        functools.partial(down_grad_kernel, owned, count),
        (steps,),
        [pl.BlockSpec((rows, hidden // steps), lambda i: (0, i))] * count + [fixed(rows, width)] * count,
        pl.BlockSpec((block, hidden), lambda i: (i, 1)),
        shape((width, 2 * hidden), BF),
        2 * count * rows * width * hidden,
        2 * count * rows * (width + hidden) + 2 * width * hidden,
    )(*acts, *ogs)


def up_grad(xs, pres, packed, block=256):
    count, (rows, width), hidden = len(xs), xs[0].shape, pres[0].shape[1]
    return pl.pallas_call(
        functools.partial(up_grad_kernel, count),
        grid=(width // block,),
        in_specs=[pl.BlockSpec((rows, block), lambda i: (0, i))] * count
        + [fixed(rows, hidden)] * count
        + [pl.BlockSpec(memory_space=pl.ANY)],
        out_specs=pl.BlockSpec((block, hidden), lambda i: (i, 0)),
        out_shape=shape((width, 2 * hidden), BF),
        input_output_aliases={2 * count: 0},
        compiler_params=pltpu.CompilerParams(vmem_limit_bytes=VMEM_BYTES),
        cost_estimate=pl.CostEstimate(
            flops=2 * count * rows * width * hidden,
            bytes_accessed=2 * count * rows * (width + hidden) + 2 * width * hidden,
            transcendentals=0,
        ),
    )(*xs, *pres, packed)


def deal(here, part, keep_ref, send_ref, at):
    rows, n = keep_ref.shape[1], part.shape[1]
    first = here[2] == 0
    for q in range(keep_ref.shape[0]):
        top, low = part[2 * q * rows : (2 * q + 1) * rows], part[(2 * q + 1) * rows : (2 * q + 2) * rows]
        keep_ref[q, :, at : at + n] = jnp.where(first, top, low)
        send_ref[q, :, at : at + n] = jnp.where(first, low, top)


def out_grad_kernel(group, per_part, here, *refs):
    atts, (branch_ref, keep_ref, send_ref) = refs[:group], refs[group:]
    owner = lax.div(pl.program_id(0), per_part)
    att = pick([a[...] for a in atts], lax.rem(owner - here[3] + group, group))
    deal(here, mm(att, branch_ref[...], TN).astype(BF), keep_ref, send_ref, 0)


def project_out_grad(here, lines, atts, branch, block=256):
    rows, depth = branch.shape
    group = len(atts)
    owned = depth // (2 * lines.chips)
    block = min(block, depth // group)
    per_part = depth // group // block
    out = pl.BlockSpec((block // (2 * owned), owned, depth), lambda i, h: (i, 0, 0))
    return call(
        functools.partial(out_grad_kernel, group, per_part),
        (depth // block,),
        [pl.BlockSpec((rows, block), lambda i, h: (0, lax.rem(i, per_part)))] * group + [fixed(rows, depth)],
        [out, out],
        [shape((lines.chips, owned, depth), BF)] * 2,
        2 * rows * depth * depth,
        2 * depth * (2 * rows + depth),
        scalars=1,
    )(here, *atts, branch)


def project_grad_kernel(here, x_ref, dq_ref, dk_ref, dv_ref, small_ref, keep_ref, send_ref):
    x, at = x_ref[...], 0
    for ref in (dq_ref, dk_ref, dv_ref):
        deal(here, mm(x, ref[...], TN).astype(BF), keep_ref, send_ref, at)
        at += ref.shape[1]
    deal(here, small_ref[...].T.astype(BF), keep_ref, send_ref, at)


def project_grad(here, lines, x, grads, small, block=512):
    rows, depth = x.shape
    width = grads[0].shape[1]
    owned = depth // (2 * lines.chips)
    columns = 3 * width + SMALL
    cols = lambda i, h: (0, i)
    out = pl.BlockSpec((block // (2 * owned), owned, columns), lambda i, h: (i, 0, 0))
    return call(
        project_grad_kernel,
        (depth // block,),
        [pl.BlockSpec((rows, block), cols)] + [fixed(rows, width)] * 3 + [pl.BlockSpec((SMALL, block), cols)],
        [out, out],
        [shape((lines.chips, owned, columns), BF)] * 2,
        6 * rows * depth * width,
        2 * rows * (depth + 3 * width) + 2 * depth * columns,
        scalars=1,
    )(here, x, *grads, small)


def after(values, *earlier):
    return lax.optimization_barrier((values, earlier))[0]


def on_device(
    lines, tokens, positions, ln1_gain, ln1_bias, qkv_weight, qkv_bias, out_weight, out_bias,
    ln2_gain, ln2_bias, fc1_weight, fc1_bias, fc2_weight, fc2_bias, out_grad,
):
    rows, width = tokens.shape[1], tokens.shape[2]
    depth = qkv_weight.shape[0]
    owners, group = width // depth, lax.axis_size(SEQ)
    side, here = lax.axis_index(SEQ), lines.here()
    others = range(1, group)
    heads = width // group
    hidden_owned = fc2_weight.shape[0] // group
    hidden_width = hidden_owned * owners
    packs = hidden_owned % depth == 0

    def gather(values):
        return lax.all_gather(values, SHARD, axis=0, tiled=True)

    def scatter(values):
        return lax.psum_scatter(values, SHARD, scatter_dimension=0, tiled=True)

    def to_next(values, d):
        return lax.ppermute(values, SEQ, shifted(group, d))

    def spread(values):
        return [values] + [to_next(values, d) for d in others]

    def in_order(parts):
        stacked = jnp.stack(parts)
        return [take(stacked, (k - side) % group, 0) for k in range(group)]

    spots = positions[:, 0, :].astype(BF).reshape(-1)
    lines_of = -(-spots.size // width)
    spots = jnp.pad(spots, (0, -(-lines_of // 16) * 16 * width - spots.size)).reshape(-1, width)
    clip = spread(jnp.concatenate([tokens[0], spots], axis=0))
    places = [v[rows:].reshape(-1)[: 3 * rows].reshape(3, rows).astype(F32) for v in clip]
    tables = rotary_tables(jnp.concatenate(places, axis=1))
    normal_one, _ = normalise(jnp.concatenate([v[:rows] for v in clip], axis=0).astype(F32))

    names = (ln1_gain, ln1_bias, out_bias, ln2_gain, ln2_bias, fc2_bias, qkv_bias, fc1_bias)
    counts = [p.size // depth for p in names]
    if packs:
        own_att, own_feed = share(here, group, qkv_weight, fc1_weight, fc2_weight, out_weight, names)
        w_up = w_down = w_out = gather(own_feed)
        out_at = 2 * hidden_width // width
    else:
        own_qkv = take(qkv_weight.reshape(depth, 3, group, heads), side, 2).reshape(depth, 3 * heads)
        extra = jnp.concatenate([p.reshape(-1, depth).T for p in names], axis=1)
        own_att = jnp.concatenate([own_qkv, jnp.pad(extra, ((0, 0), (0, SMALL - sum(counts))))], axis=1)
        own_up = take(fc1_weight.reshape(depth, owners, group, hidden_owned), side, 2).reshape(depth, -1)
        own_down = take(fc2_weight.reshape(group, hidden_owned, width), side, 0)
        w_up, w_down, w_out, out_at = gather(own_up), gather(own_down), gather(out_weight), 0
    qkv_mine, qkv_sib = staged_gather(lines, here, own_att, (tables, normal_one))
    grads = spread(out_grad[0])

    small = [p[:, :, 3 * heads :].astype(F32) for p in (qkv_mine, qkv_sib)]
    pair = [jnp.where(here[2] == 0, small[0], small[1]), jnp.where(here[2] == 0, small[1], small[0])]
    rows_of = jnp.stack(pair, axis=1).reshape(width, SMALL).T[: sum(counts)]
    vectors, at = [], 0
    for n in counts:
        vectors.append(rows_of[at : at + n].reshape(n, owners, depth).transpose(1, 0, 2).reshape(1, -1))
        at += n
    gain_one, bias_one, b_out, gain_two, bias_two, b_down, b_qkv, b_up = vectors
    b_qkv = take(b_qkv.reshape(3, group, heads), side, 1).reshape(1, -1)
    b_up = take(b_up.reshape(owners, group, hidden_owned), side, 1).reshape(1, -1)

    normed_one = (normal_one * gain_one + bias_one).astype(BF)
    qkv, w_qkv = project(here, normed_one, qkv_mine, qkv_sib, b_qkv, tables, heads)
    att, lse = attend(qkv)

    att = after(att, grads)
    atts = [att] + [to_next(att[d * rows : (d + 1) * rows], -d) for d in others]
    hidden, normed_two = project_out(here, atts, w_out, out_at, tokens[0], b_out, gain_two, bias_two)
    normed = spread(normed_two)

    fed = [None] * group
    for d in range(group):
        x = after(normed[d], fed[0][2]) if d else normed[0]
        fed[d] = feed(x, grads[d], w_up, w_down, packs, b_up, depth, F32 if d == 0 else BF)
    acts, pres, dns, outs, sums = zip(*fed)
    dn_far = [to_next(dns[d], -d) for d in others]
    out_far = [to_next(outs[d], -d) for d in others]
    dn_own = dns[0]
    if packs:
        fed_grads = down_grad(acts, grads, depth)
        fed_grads = up_grad(normed, pres, fed_grads)
        dn_own = after(dn_own, fed_grads)
    hidden_grad, branch, sums_two, *shares = hidden_back(
        here, dn_own, dn_far, hidden, out_grad[0], gain_two, w_out, out_at
    )
    if packs:
        fed_sum = scatter(fed_grads)
    att_grads = jnp.concatenate([shares[0]] + [to_next(shares[d], d) for d in others], axis=0)

    out_sum = StagedSum(lines, here, *project_out_grad(here, lines, atts, branch))
    att_grads = after(att_grads, out_sum.short())

    *qkv_grads, sums_qkv = attend_back(qkv, att, lse, att_grads, tables)
    qkv_grads = after(qkv_grads, (out_far, out_sum.arrived))

    own = (jnp.arange(group) == side).astype(F32)
    qkv_b = sums_qkv[:3, None, :] * own[None, :, None]
    up_b = functools.reduce(jnp.add, sums).reshape(owners, 1, hidden_owned) * own[None, :, None]
    vectors = (jnp.zeros((2, width), F32), sums_two[2], sums_two[0], sums_two[1], sums_two[3], qkv_b, up_b)
    rows_of = [vectors[0]]
    rows_of += [v.reshape(owners, n, depth).transpose(1, 0, 2).reshape(n, width) for v, n in zip(vectors[1:], counts[2:])]
    rows_of = jnp.pad(jnp.concatenate(rows_of, axis=0), ((0, SMALL - sum(counts)), (0, 0)))
    qkv_sum = StagedSum(lines, here, *project_grad(here, lines, normed_one, qkv_grads, rows_of))

    back = [None] * group
    before = qkv_sum.keep
    for d in list(others) + [0]:
        back[d] = project_back(after(qkv_grads, before), w_qkv, clip[d], d, rows, F32 if d == 0 else BF)
        if d == group - 1:
            qkv_sum.keep = after(qkv_sum.keep, back[d][0])
            before = qkv_sum.short()
    dn_one, sums_one = zip(*back)
    dn_one_far = [to_next(dn_one[d], -d) for d in others]
    sums_one = functools.reduce(jnp.add, sums_one)
    sums_one = sums_one + lax.ppermute(sums_one, "c", shifted(2, 1))
    sums_one = functools.reduce(
        jnp.add, [sums_one] + [lax.ppermute(sums_one, lines.short, shifted(lines.n_short, d)) for d in range(1, lines.n_short)]
    )
    late = sums_one[:2].reshape(2, lines.outer, lines.inner, 2, depth)
    late = take(take(late, here[2], 3), here[1], 2 if lines.outer_long else 1)
    late = jnp.pad(late.transpose(1, 2, 0), ((0, 0), (0, 0), (0, SMALL - 2)))
    out_sum.arrived = after(out_sum.arrived, before)
    out_sum.long()
    qkv_sum.long((late,))
    tokens_grad = tokens_back(dn_one[0], dn_one_far, tokens[0], hidden_grad, gain_one)
    block_out = hidden + outs[0] + b_down
    for far in out_far:
        block_out = block_out + far.astype(F32)
    block_out = block_out.astype(BF)

    def from_next(values):
        return [values] + [to_next(values, -d) for d in others]

    if packs:
        up_total, down_total = finish_feed(here, from_next(fed_sum), fc1_weight.shape, fc2_weight.shape)
    else:
        up_sum = scatter(functools.reduce(jnp.add, [mm(x, p, TN) for x, p in zip(normed, pres)]).astype(BF))
        down_sum = scatter(functools.reduce(jnp.add, [mm(a, g, TN) for a, g in zip(acts, grads)]).astype(BF))
        shares = [v.reshape(depth, owners, hidden_owned) for v in in_order(from_next(up_sum))]
        up_total = jnp.stack(shares, axis=2).reshape(depth, -1).astype(F32)
        down_total = jnp.concatenate(in_order(from_next(down_sum)), axis=0).astype(F32)
    out_last = out_sum.last()
    qkv_sum.parts = after(qkv_sum.parts, (tokens_grad, block_out, up_total, down_total, out_last))
    att_sums = jnp.concatenate([out_last, qkv_sum.last()], axis=1)
    out_total, qkv_total, rows_of = finish_attention(here, from_next(att_sums), width)

    ends = np.cumsum(counts)
    g1, b1, bo, g2, b2, bd, bq, bu = [rows_of[e - n : e].reshape(-1) for e, n in zip(ends, counts)]
    return (
        block_out[None], tokens_grad[None], g1, b1, qkv_total, bq, out_total, bo, g2, b2, up_total, bu,
        down_total, bd,
    )


def solution(mesh):
    lines = Lines(mesh)
    vector, matrix, tokens = P(SHARD), P(SHARD, None), P(SHARD, SEQ, None)
    return jax.shard_map(
        functools.partial(on_device, lines),
        mesh=lines.mesh,
        in_specs=(
            tokens, P(None, SHARD, SEQ), vector, vector, matrix, vector, matrix, vector, vector, vector, matrix, vector,
            matrix, vector, tokens,
        ),
        out_specs=(
            tokens, tokens, vector, vector, matrix, vector, matrix, vector, vector, vector, matrix, vector, matrix, vector
        ),
        check_vma=False,
    )
```

```python
import functools

import jax
import jax.numpy as jnp
import numpy as np
from jax import lax
from jax.experimental import pallas as pl
from jax.experimental.pallas import tpu as pltpu
from jax.sharding import Mesh, PartitionSpec as P

HD = 64
EPS = 1e-06
THETA = 10000.0
LOG2E = 1.4426950408889634
SCALE = HD**-0.5
BF = jnp.bfloat16
F32 = jnp.float32
NT = (((1,), (1,)), ((), ()))
TN = (((0,), (0,)), ((), ()))
NN = (((1,), (0,)), ((), ()))
SMALL = 128
VMEM_BYTES = 56 << 20
LOW, HIGH = 0.25, 200
SHARD = ("o", "i", "c")
SEQ = "seq"


def mm(a, b, dims=NN):
    return lax.dot_general(a, b, dims, preferred_element_type=F32)


def shifted(size, by):
    return [(i, (i + by) % size) for i in range(size)]


def take(values, index, axis):
    return lax.dynamic_index_in_dim(values, index, axis, keepdims=False)


def shape(dims, dtype):
    return jax.ShapeDtypeStruct(dims, dtype)


def fixed(*dims):
    return pl.BlockSpec(dims, lambda *_: (0,) * len(dims))


def spec(block, index):
    return pl.BlockSpec(block, index)


def call(kernel, grid, in_specs, out_specs, out_shape, flops, moved, exps=0, scratch=(), scalars=0, weight=LOW):
    return pl.pallas_call(
        kernel,
        grid_spec=pltpu.PrefetchScalarGridSpec(
            num_scalar_prefetch=scalars,
            grid=grid,
            in_specs=in_specs,
            out_specs=out_specs,
            scratch_shapes=list(scratch),
        ),
        out_shape=out_shape,
        compiler_params=pltpu.CompilerParams(vmem_limit_bytes=VMEM_BYTES),
        cost_estimate=pl.CostEstimate(flops=int(weight * flops), bytes_accessed=int(weight * moved), transcendentals=int(weight * exps)),
    )


def pick(parts, index):
    chosen = parts[0]
    for k in range(1, len(parts)):
        chosen = jnp.where(index == k, parts[k], chosen)
    return chosen


def chips_in_line(mesh):
    chips = mesh.devices.shape[0] // 2
    places = [getattr(d, "coords", None) for d in mesh.devices[::2, 0]]
    if places[0] is None or chips < 2:
        return 2 if chips % 2 == 0 else 1
    axis = [a for a in range(3) if places[0][a] != places[1][a]][0]
    inner = 1
    while inner < chips and all(places[inner][a] == places[0][a] for a in range(3) if a != axis):
        inner += 1
    return inner


class Lines:
    def __init__(self, mesh):
        fsdp, seq = mesh.devices.shape
        self.chips = fsdp // 2
        self.inner = chips_in_line(mesh)
        self.outer = self.chips // self.inner
        self.mesh = Mesh(mesh.devices.reshape(self.outer, self.inner, 2, seq), SHARD + (SEQ,))
        self.outer_long = self.outer >= self.inner
        self.long, self.short = ("o", "i") if self.outer_long else ("i", "o")
        self.n_long, self.n_short = max(self.outer, self.inner), min(self.outer, self.inner)

    def place(self, long, short):
        return (long, short) if self.outer_long else (short, long)

    def split(self, values):
        return values.reshape(self.outer, self.inner, *values.shape[1:])

    def here(self):
        return jnp.stack([lax.axis_index(a) for a in (self.long, self.short, "c", SEQ)]).astype(jnp.int32)


def stack_kernel(lines, here, *refs):
    *pieces, out, sems = refs
    copies = []
    for n, piece in enumerate(pieces):
        back_short, back_long = n // lines.n_long, n % lines.n_long
        long = lax.rem(here[0] + (lines.n_long - back_long), lines.n_long)
        short = lax.rem(here[1] + (lines.n_short - back_short), lines.n_short)
        a, b = lines.place(long, short)
        copies.append(pltpu.make_async_copy(piece, out.at[a, b], sems.at[n]))
    for copy in copies:
        copy.start()
    for copy in copies:
        copy.wait()


def staged_gather(lines, here, values, meanwhile):
    line = [values] + [lax.ppermute(values, lines.long, shifted(lines.n_long, d)) for d in range(1, lines.n_long)]
    pieces = list(line)
    for d in range(1, lines.n_short):
        pieces += [lax.ppermute(v, lines.short, shifted(lines.n_short, d)) for v in line]
    dims = (lines.outer, lines.inner) + values.shape
    pieces = after(pieces, meanwhile)
    mine = call(
        functools.partial(stack_kernel, lines),
        (1,),
        [pl.BlockSpec(memory_space=pl.ANY)] * len(pieces),
        pl.BlockSpec(dims, lambda *_: (0,) * 4),
        shape(dims, values.dtype),
        0,
        4 * lines.chips * values.size,
        scratch=[pltpu.SemaphoreType.DMA((len(pieces),))],
        scalars=1,
    )(here, *pieces)
    mine = mine.reshape((lines.chips,) + values.shape)
    return mine, lax.ppermute(mine, "c", shifted(2, 1))


def add_first_kernel(here, keep_ref, got_ref, out_ref):
    out_ref[...] = (keep_ref[...].astype(F32) + got_ref[...].astype(F32)).astype(BF)


def add_second_kernel(lines, late, here, keep_ref, got_ref, *refs):
    ins, refs = refs[: lines.n_short - 1], refs[lines.n_short - 1 :]
    late_ref, outs = (refs[0], refs[1:]) if late else (None, refs)
    for k, out in enumerate(outs):
        at = lines.place(lax.rem(here[0] + k, lines.n_long), 0)
        total = keep_ref[at].astype(F32) + got_ref[at].astype(F32)
        for r in ins:
            total = total + r[at].astype(F32)
        if late:
            n = total.shape[1] - SMALL
            out[:, :n] = total[:, :n].astype(BF)
            out[:, n:] = (total[:, n:] + late_ref[at[0] + at[1]]).astype(BF)
        else:
            out[...] = total.astype(BF)


def add_last_kernel(*refs):
    *ins, out = refs
    out[...] = functools.reduce(jnp.add, [r[...].astype(F32) for r in ins]).astype(BF)


class StagedSum:
    def __init__(self, lines, here, keep, send):
        self.lines, self.here = lines, here
        self.got = lines.split(lax.ppermute(send, "c", shifted(2, 1)))
        self.keep = lines.split(keep)
        self.rows, self.columns = keep.shape[1:]
        self.dims = lines.place(lines.n_long, 1) + (self.rows, self.columns)
        self.size = lines.n_long * self.rows * self.columns

    def across(self, d):
        lines = self.lines
        return pl.BlockSpec(self.dims, lambda i, h: lines.place(0, lax.rem(h[1] + d, lines.n_short)) + (0, 0))

    def short(self):
        lines, dims = self.lines, self.dims
        away = [
            call(
                add_first_kernel,
                (1,),
                [self.across(d)] * 2,
                pl.BlockSpec(dims, lambda i, h: (0, 0, 0, 0)),
                shape(dims, BF),
                self.size,
                6 * self.size,
                scalars=1,
            )(self.here, self.keep, self.got)
            for d in range(1, lines.n_short)
        ]
        self.arrived = [lax.ppermute(v, lines.short, shifted(lines.n_short, d + 1)) for d, v in enumerate(away)]
        return away

    def long(self, late=()):
        lines = self.lines
        flat = pl.BlockSpec((self.rows, self.columns), lambda i, h: (0, 0))
        parts = call(
            functools.partial(add_second_kernel, lines, len(late) > 0),
            (1,),
            [self.across(0)] * 2
            + [pl.BlockSpec(self.dims, lambda i, h: (0, 0, 0, 0))] * len(self.arrived)
            + [fixed(*v.shape) for v in late],
            [flat] * lines.n_long,
            [shape((self.rows, self.columns), BF)] * lines.n_long,
            3 * self.size,
            8 * self.size,
            scalars=1,
        )(self.here, self.keep, self.got, *self.arrived, *late)
        self.parts = [parts[0]]
        self.parts += [lax.ppermute(parts[d], lines.long, shifted(lines.n_long, d)) for d in range(1, lines.n_long)]
        return parts

    def last(self):
        return call(
            add_last_kernel,
            (1,),
            [fixed(self.rows, self.columns)] * len(self.parts),
            fixed(self.rows, self.columns),
            shape((self.rows, self.columns), BF),
            self.size,
            3 * self.size,
        )(*self.parts)


def share_kernel(group, here, qkv_ref, up_ref, down_ref, out_ref, *refs):
    *small_refs, att_ref, feed_ref = refs
    side = here[3]
    depth, width = out_ref.shape
    heads = width // group
    for k in range(3):
        parts = [qkv_ref[:, k * width + g * heads : k * width + (g + 1) * heads] for g in range(group)]
        att_ref[:, k * heads : (k + 1) * heads] = pick(parts, side)
    rows = [r[j : j + depth].astype(F32).reshape(1, depth) for r in small_refs for j in range(0, r.shape[0], depth)]
    rows.append(jnp.zeros((SMALL - len(rows), depth), F32))
    att_ref[:, 3 * heads :] = jnp.concatenate(rows, axis=0).T.astype(BF)
    owned = down_ref.shape[0] // group
    hidden = up_ref.shape[1] // group
    for f in range(hidden // owned):
        parts = [up_ref[:, (f * group + g) * owned : (f * group + g + 1) * owned] for g in range(group)]
        feed_ref[:, f * owned : (f + 1) * owned] = pick(parts, side)
    for j in range(owned // depth):
        parts = [down_ref[g * owned + j * depth : g * owned + (j + 1) * depth, :] for g in range(group)]
        feed_ref[:, hidden + j * width : hidden + (j + 1) * width] = pick(parts, side)
    feed_ref[:, 2 * hidden :] = out_ref[...]


def share(here, group, qkv, up, down, out, small):
    depth, width = out.shape
    args = (qkv, up, down, out, *small)
    att, feed_columns = qkv.shape[1] // group + SMALL, 2 * up.shape[1] // group + width
    return call(
        functools.partial(share_kernel, group),
        (1,),
        [fixed(*a.shape) for a in args],
        [fixed(depth, att), fixed(depth, feed_columns)],
        [shape((depth, att), BF), shape((depth, feed_columns), BF)],
        0,
        8 * depth * (att + feed_columns),
        scalars=1,
    )(here, *args)


def finish_attention_kernel(group, here, *refs):
    shares, (out_ref, qkv_ref, *vector_refs) = refs[:group], refs[group:]
    width = out_ref.shape[1]
    heads = width // group
    total = functools.reduce(jnp.add, [r[:, :width].astype(F32) for r in shares])
    out_ref[...] = total
    small = functools.reduce(jnp.add, [r[:, -SMALL:].astype(F32) for r in shares])
    small, row = small.T, 0
    for ref in vector_refs:
        for at in range(0, ref.shape[0], small.shape[1]):
            ref[at : at + small.shape[1]] = small[row]
            row += 1
    for k in range(group):
        source = lax.rem(k - here[3] + group, group)
        for m in range(3):
            at, start = m * width + k * heads, width + m * heads
            parts = [r[:, start : start + heads] for r in shares]
            qkv_ref[:, at : at + heads] = pick(parts, source).astype(F32)


def finish_attention(here, shares, width, counts):
    depth, group = shares[0].shape[0], len(shares)
    return call(
        functools.partial(finish_attention_kernel, group),
        (1,),
        [fixed(*v.shape) for v in shares],
        [fixed(depth, width), fixed(depth, 3 * width)] + [fixed(n * depth) for n in counts],
        [shape((depth, width), F32), shape((depth, 3 * width), F32)] + [shape((n * depth,), F32) for n in counts],
        0,
        24 * depth * width,
        scalars=1,
    )(here, *shares)


def finish_feed_kernel(group, here, *refs):
    shares, (up_ref, down_ref) = refs[:group], refs[group:]
    depth, width = shares[0].shape[0], down_ref.shape[1]
    owned = down_ref.shape[0] // group
    hidden = up_ref.shape[1] // group
    for k in range(group):
        source = lax.rem(k - here[3] + group, group)
        for f in range(hidden // owned):
            at = (f * group + k) * owned
            up_ref[:, at : at + owned] = pick([r[:, f * owned : (f + 1) * owned] for r in shares], source).astype(F32)
        for j in range(owned // depth):
            at, start = k * owned + j * depth, hidden + j * width
            down_ref[at : at + depth, :] = pick([r[:, start : start + width] for r in shares], source).astype(F32)


def finish_feed(here, shares, up_shape, down_shape):
    return call(
        functools.partial(finish_feed_kernel, len(shares)),
        (1,),
        [fixed(*v.shape) for v in shares],
        [fixed(*up_shape), fixed(*down_shape)],
        [shape(up_shape, F32), shape(down_shape, F32)],
        0,
        12 * up_shape[0] * up_shape[1],
        scalars=1,
    )(here, *shares)


def rotated(values, cos, low, high):
    half = 2 * (HD // 3 // 2) // 2
    return values * cos + pltpu.roll(values, values.shape[1] - half, 1) * low + pltpu.roll(values, half, 1) * high


def project_kernel(group, here, *refs):
    clip, refs = refs[:group], refs[group:]
    mine_ref, sib_ref, mine_small, sib_small, cos_ref, low_ref, high_ref, out_ref, w_ref, x_ref, lines_ref, bias = refs
    rows = mine_ref.shape[1]
    core, side, step = here[2], here[3], pl.program_id(0)
    width = out_ref.shape[1]

    @pl.when(step == 0)
    def _():
        owners = []
        for q in range(mine_small.shape[0]):
            a, b = mine_small[q].astype(F32), sib_small[q].astype(F32)
            owners += [jnp.where(core == 0, a, b), jnp.where(core == 0, b, a)]
        lines = jnp.concatenate(owners, axis=0).T[: lines_ref.shape[0]]
        lines_ref[...] = lines
        count = width // rows
        for k in range(3):
            for j in range(count):
                at = [(k * group + g) * count + j for g in range(group)]
                parts = [lines[6 + p % 3 : 7 + p % 3, p // 3 * rows : (p // 3 + 1) * rows] for p in at]
                bias[k : k + 1, j * rows : (j + 1) * rows] = pick(parts, side)
        tokens = clip[0].shape[0]
        block = min(256, tokens)
        for d, ref in enumerate(clip):
            for r in range(0, tokens, block):
                normal, _ = normalise(ref[r : r + block, :].astype(F32))
                at = d * tokens + r
                x_ref[at : at + block, :] = (normal * lines[0:1] + lines[1:2]).astype(BF)

    for q in range(mine_ref.shape[0]):
        w_ref[pl.ds(pl.multiple_of((2 * q + core) * rows, rows), rows), :] = mine_ref[q]
        w_ref[pl.ds(pl.multiple_of((2 * q + 1 - core) * rows, rows), rows), :] = sib_ref[q]
    values = mm(x_ref[...], w_ref[...]) + bias[pl.ds(step, 1), :]

    @pl.when(step < 2)
    def _():
        cos, low, high = cos_ref[...], low_ref[...], high_ref[...]
        for j in range(0, width, 128):
            out_ref[:, j : j + 128] = rotated(values[:, j : j + 128], cos, low, high).astype(BF)

    @pl.when(step >= 2)
    def _():
        out_ref[...] = values.astype(BF)


def project(here, clip, tokens, mine, sib, tables, width):
    depth, group = clip[0].shape[1], len(clip)
    rows = tokens * group
    part = pl.BlockSpec(mine.shape[:2] + (width,), lambda i, h: (0, 0, i))
    small = pl.BlockSpec(mine.shape[:2] + (SMALL,), lambda i, h: (0, 0, 3 * width // SMALL))
    return call(
        functools.partial(project_kernel, group),
        (3,),
        [fixed(tokens, depth)] * group + [part, part, small, small] + [fixed(rows, 128)] * 3,
        [
            pl.BlockSpec((rows, width), lambda i, h: (0, i)),
            pl.BlockSpec((depth, width), lambda i, h: (0, i)),
            fixed(rows, depth),
            fixed(16, depth),
        ],
        [shape((rows, 3 * width), BF), shape((depth, 3 * width), BF), shape((rows, depth), BF), shape((16, depth), F32)],
        6 * rows * depth * width,
        12 * depth * width + 2 * rows * (depth + 3 * width),
        scratch=[pltpu.VMEM((8, width), F32)],
        scalars=1,
    )(here, *clip, mine, sib, mine, sib, *tables)


def rotary_tables(positions):
    width = 2 * (HD // 3 // 2)
    half = width // 2
    freqs = np.power(np.float32(THETA), -(np.arange(half, dtype=np.float32) * np.float32(2.0 / width)))
    column = np.arange(2 * HD) % HD
    turns = column < 3 * width
    axis = np.minimum(column // width, 2)
    freq = np.where(turns, freqs[column % half], 0.0).astype(np.float32)
    leading = turns & (column % width < half)
    trailing = turns & (column % width >= half)
    place = jnp.where(axis == 0, positions[0][:, None], jnp.where(axis == 1, positions[1][:, None], positions[2][:, None]))
    angle = place * freq
    sine = jnp.sin(angle)
    return jnp.cos(angle), jnp.where(leading, -sine, 0.0), jnp.where(trailing, sine, 0.0)


def over_blocks(rows, block, step):
    if rows // block <= 4:
        for i in range(rows // block):
            step(pl.ds(i * block, block))
    else:

        def body(i, carry):
            step(pl.ds(pl.multiple_of(i * block, block), block))
            return carry

        lax.fori_loop(0, rows // block, body, 0)


def attend_kernel(block, q_ref, k_ref, v_ref, o_ref, lse_ref):
    rows = q_ref.shape[0]
    first = lax.broadcasted_iota(jnp.int32, (1, 128), 1) < HD
    masks = (first, jnp.logical_not(first))
    factor = jnp.float32(SCALE * LOG2E)
    zero, one = jnp.zeros((), BF), jnp.ones((), BF)

    def scores_of(rs, h):
        return mm(jnp.where(masks[h], q_ref[rs, :], zero), k_ref[...], NT)

    def finish(scores, h):
        peak = jnp.max(scores, axis=1, keepdims=True) * factor
        weights = jnp.exp2(scores * factor - peak).astype(BF)
        out = mm(weights, jnp.where(masks[h], v_ref[...], one))
        total = out[:, (1 - h) * HD : (1 - h) * HD + 1]
        return out * (1.0 / total), peak + jnp.log2(total)

    def store(rs, left, right):
        o_ref[rs, :] = jnp.where(first, left[0], right[0]).astype(BF)
        lse_ref[rs, :] = jnp.where(first, left[1], right[1])

    if rows // block <= 4:
        places = [pl.ds(i * block, block) for i in range(rows // block)]
        turns = [(rs, h) for rs in places for h in range(2)]
        scores, done = scores_of(*turns[0]), []
        for n, (rs, h) in enumerate(turns):
            ahead = scores_of(*turns[n + 1]) if n + 1 < len(turns) else None
            done.append(finish(scores, h))
            if h == 1:
                store(rs, *done[-2:])
            scores = ahead
    else:
        over_blocks(rows, block, lambda rs: store(rs, *[finish(scores_of(rs, h), h) for h in range(2)]))


def attend_back_kernel(
    block, q_ref, k_ref, v_ref, o_ref, lse_ref, do_ref, cos_ref, low_ref, high_ref, dq_ref, dk_ref, dv_ref, sums_ref, dk_sum, dv_sum
):
    rows = q_ref.shape[0]
    first = lax.broadcasted_iota(jnp.int32, (1, 128), 1) < HD
    masks = (first, jnp.logical_not(first))
    factor = jnp.float32(SCALE * LOG2E)
    zero = jnp.zeros((), BF)
    dk_sum[...] = jnp.zeros_like(dk_sum)
    dv_sum[...] = jnp.zeros_like(dv_sum)

    def step(rs):
        q, do = q_ref[rs, :], do_ref[rs, :]
        od = (o_ref[rs, :].astype(F32) * do.astype(F32)).T
        lse = lse_ref[rs, :].T
        dq = None
        for h, mine in enumerate(masks):
            qh, doh, k = jnp.where(mine, q, zero), jnp.where(mine, do, zero), k_ref[...]
            delta = jnp.sum(od[h * HD : (h + 1) * HD, :], axis=0, keepdims=True)
            p = jnp.exp2(mm(k, qh, NT) * factor - lse[h * HD : h * HD + 1, :])
            ds = (p * (mm(v_ref[...], doh, NT) - delta)).astype(BF)
            dv_sum[...] += mm(p.astype(BF), doh)
            dk_sum[...] += mm(ds, qh)
            part = mm(jnp.where(mine, k, zero), ds, TN)
            dq = part if dq is None else dq + part
        dq = (dq.T * SCALE).astype(BF).astype(F32)
        dq_ref[rs, :] = rotated(dq, cos_ref[rs, :], -low_ref[rs, :], -high_ref[rs, :]).astype(BF)

    over_blocks(rows, block, step)
    dk = (dk_sum[...] * SCALE).astype(BF).astype(F32)
    dk_ref[...] = rotated(dk, cos_ref[...], -low_ref[...], -high_ref[...]).astype(BF)
    dv_ref[...] = dv_sum[...].astype(BF)
    sums = [jnp.sum(r[...].astype(F32), axis=0, keepdims=True) for r in (dq_ref, dk_ref, dv_ref)]
    sums_ref[...] = jnp.concatenate(sums + [jnp.zeros((5, 128), F32)], axis=0)


def pair_spec(rows, first=0):
    return pl.BlockSpec((rows, 128), lambda i: (0, first + i))


def attend(qkv, block=512):
    rows, columns = qkv.shape[0], qkv.shape[1] // 3
    pairs = columns // 128
    return call(
        functools.partial(attend_kernel, min(block, (1 << 19) // rows)),
        (pairs,),
        [pair_spec(rows, k * pairs) for k in range(3)],
        [pair_spec(rows)] * 2,
        [shape((rows, columns), BF), shape((rows, columns), F32)],
        16 * rows * rows * columns,
        rows * columns * 12,
        rows * rows * columns // HD,
    )(qkv, qkv, qkv)


def attend_back(qkv, o, lse, do, tables, block=512):
    rows, columns = o.shape
    pairs = columns // 128
    return call(
        functools.partial(attend_back_kernel, min(block, (1 << 19) // rows)),
        (pairs,),
        [pair_spec(rows, k * pairs) for k in range(3)] + [pair_spec(rows)] * 3 + [fixed(rows, 128)] * 3,
        [pair_spec(rows)] * 3 + [pl.BlockSpec((8, 128), lambda i: (0, i))],
        [shape((rows, columns), BF)] * 3 + [shape((8, columns), F32)],
        40 * rows * rows * columns,
        rows * columns * 20,
        rows * rows * columns // HD,
        [pltpu.VMEM((rows, 128), F32)] * 2,
    )(qkv, qkv, qkv, o, lse, do, *tables)


def normalise(values):
    center = values - jnp.mean(values, axis=-1, keepdims=True)
    factor = lax.rsqrt(jnp.mean(center * center, axis=-1, keepdims=True) + EPS)
    return center * factor, factor


def normalise_back(grads, gain, normal, factor):
    e = grads * gain
    inner = e - jnp.mean(e, axis=-1, keepdims=True) - normal * jnp.mean(e * normal, axis=-1, keepdims=True)
    return factor * inner


def column_sums(out_ref, *parts):
    sums = [jnp.sum(p, axis=0, keepdims=True) for p in parts]
    sums.append(jnp.zeros((8 - len(sums), sums[0].shape[1]), F32))
    block = jnp.concatenate(sums, axis=0)

    @pl.when(pl.program_id(0) == 0)
    def _():
        out_ref[...] = block

    @pl.when(pl.program_id(0) > 0)
    def _():
        out_ref[...] += block


def out_kernel(group, here, *refs):
    atts, weights, (tokens_ref, b_ref, gain_ref, bias_ref, hidden_ref, normed_ref) = (
        refs[:group],
        refs[group : 2 * group],
        refs[2 * group :],
    )
    hidden = tokens_ref[...].astype(F32) + b_ref[...]
    for att, w in zip(atts, weights):
        hidden = hidden + mm(att[...], w[...])
    hidden_ref[...] = hidden
    normed_ref[...] = (normalise(hidden)[0] * gain_ref[...] + bias_ref[...]).astype(BF)


def project_out(here, atts, weight, at, tokens, b, gain, bias, block=256):
    rows, width = tokens.shape
    group, heads = len(atts), atts[0].shape[1]
    row = pl.BlockSpec((block, width), lambda i, h: (i, 0))
    return call(
        functools.partial(out_kernel, group),
        (rows // block,),
        [pl.BlockSpec((block, heads), lambda i, h: (i, 0))] * group
        + [pl.BlockSpec((heads, width), lambda i, h, d=d: (lax.rem(h[3] + d, group), at)) for d in range(group)]
        + [row]
        + [fixed(1, width)] * 3,
        [row, row],
        [shape((rows, width), F32), shape((rows, width), BF)],
        2 * rows * width * width,
        2 * width * width + 10 * rows * width,
        scalars=1,
    )(here, *atts, *[weight] * group, tokens, b, gain, bias)


def hidden_back_kernel(group, here, *refs):
    dn_ref, far_refs, (hidden_ref, og_ref, gain_ref, w_ref, grad_ref, branch_ref, sums_ref, *att_refs) = (
        refs[0],
        refs[1:group],
        refs[group:],
    )
    dn = dn_ref[...]
    for far in far_refs:
        dn = dn + far[...].astype(F32)
    normal, factor = normalise(hidden_ref[...])
    og = og_ref[...].astype(F32)
    grad = og + normalise_back(dn, gain_ref[...], normal, factor)
    grad_ref[...] = grad
    branch = grad.astype(BF)
    branch_ref[...] = branch
    att = mm(branch, w_ref[...], NT).astype(BF)
    heads = att.shape[1] // group
    parts = [att[:, k * heads : (k + 1) * heads] for k in range(group)]
    for d, ref in enumerate(att_refs):
        ref[...] = pick(parts, lax.rem(here[3] + d, group))
    column_sums(sums_ref, dn * normal, dn, branch.astype(F32), og)


def hidden_back(here, dn, dn_far, hidden, og, gain, weight, at, block=256):
    rows, width = hidden.shape
    group = 1 + len(dn_far)
    row = pl.BlockSpec((block, width), lambda i, h: (i, 0))
    share = pl.BlockSpec((block, width // group), lambda i, h: (i, 0))
    return call(
        functools.partial(hidden_back_kernel, group),
        (rows // block,),
        [row] * group + [row, row, fixed(1, width), pl.BlockSpec((width, width), lambda i, h: (0, at))],
        [row, row, fixed(8, width)] + [share] * group,
        [shape((rows, width), F32), shape((rows, width), BF), shape((8, width), F32)]
        + [shape((rows, width // group), BF)] * group,
        2 * rows * width * width,
        2 * width * width + 18 * rows * width,
        scalars=1,
        weight=HIGH,
    )(here, dn, *dn_far, hidden, og, gain, weight)


def tokens_back_kernel(extra, *refs):
    dn_ref, far_refs, (tokens_ref, grad_ref, gain_ref, out_ref) = refs[0], refs[1 : 1 + extra], refs[1 + extra :]
    dn = dn_ref[...]
    for far in far_refs:
        dn = dn + far[...].astype(F32)
    normal, factor = normalise(tokens_ref[...].astype(F32))
    out_ref[...] = grad_ref[...] + normalise_back(dn, gain_ref[...], normal, factor)


def tokens_back(dn, dn_far, tokens, grad, gain, block=256):
    rows, width = tokens.shape
    row = pl.BlockSpec((block, width), lambda i: (i, 0))
    return call(
        functools.partial(tokens_back_kernel, len(dn_far)),
        (rows // block,),
        [row] * (3 + len(dn_far)) + [fixed(1, width)],
        row,
        shape((rows, width), F32),
        20 * rows * width,
        14 * rows * width,
    )(dn, *dn_far, tokens, grad, gain)


def project_back_kernel(dq_ref, dk_ref, dv_ref, w_ref, tokens_ref, out_ref, sums_ref):
    width = dq_ref.shape[1]
    total = functools.reduce(
        jnp.add,
        [mm(g[...], w_ref[:, k * width : (k + 1) * width], NT) for k, g in enumerate((dq_ref, dk_ref, dv_ref))],
    )
    out_ref[...] = total.astype(out_ref.dtype)
    normal, _ = normalise(tokens_ref[...].astype(F32))
    column_sums(sums_ref, total * normal, total)


def project_back(grads, weight, tokens, piece, rows, dtype):
    width, depth = grads[0].shape[1], tokens.shape[1]
    block = rows // 2
    row = pl.BlockSpec((block, depth), lambda i: (i, 0))
    return call(
        project_back_kernel,
        (2,),
        [pl.BlockSpec((block, width), lambda i: (2 * piece + i, 0))] * 3 + [fixed(depth, 3 * width), row],
        [row, fixed(8, depth)],
        [shape((rows, depth), dtype), shape((8, depth), F32)],
        6 * rows * width * depth,
        6 * width * depth + rows * (6 * width + 6 * depth),
    )(*grads, weight, tokens)


def unpack_down(block, rows, width):
    parts = block.shape[1] // width
    if parts == 1:
        return block
    owners = block.shape[0] // rows
    return jnp.concatenate(
        [block[f * rows : (f + 1) * rows, j * width : (j + 1) * width] for f in range(owners) for j in range(parts)], axis=0
    )


def feed_kernel(owned, x_ref, og_ref, up_ref, down_ref, b_ref, act_ref, pre_ref, dn_ref, out_ref, sums_ref, dn_sum, out_sum):
    step, last = pl.program_id(0), pl.num_programs(0) - 1
    width = x_ref.shape[1]
    up = up_ref[...]
    down = unpack_down(down_ref[...], owned, width)
    u = mm(x_ref[...], up) + b_ref[...]
    phi = 0.5 * (1.0 + lax.erf(u * 0.7071067811865476))
    slope = phi + u * jnp.exp(-0.5 * u * u) * 0.3989422804014327
    act = (u * phi).astype(BF)
    act_ref[...] = act
    pre = (mm(og_ref[...], down, NT) * slope).astype(BF)
    pre_ref[...] = pre
    sums_ref[...] = jnp.sum(pre.astype(F32), axis=0, keepdims=True)
    dn = mm(pre, up, NT)
    out = mm(act, down)

    @pl.when(step == 0)
    def _():
        dn_sum[...] = dn
        out_sum[...] = out

    @pl.when(step > 0)
    def _():
        dn_sum[...] += dn
        out_sum[...] += out

    @pl.when(step == last)
    def _():
        dn_ref[...] = dn_sum[...].astype(dn_ref.dtype)
        out_ref[...] = out_sum[...].astype(out_ref.dtype)


def feed(x, og, up, down, packs, bias, owned, dtype, block=512):
    rows, width = x.shape
    hidden = bias.shape[1]
    block = min(block, hidden)
    steps = hidden // block
    down_rows = down.shape[0] // steps
    down_columns = hidden if packs else width
    columns = pl.BlockSpec((rows, block), lambda i: (0, i))
    vector = pl.BlockSpec((1, block), lambda i: (0, i))
    return call(
        functools.partial(feed_kernel, owned),
        (steps,),
        [
            fixed(rows, width),
            fixed(rows, width),
            pl.BlockSpec((width, block), lambda i: (0, i)),
            pl.BlockSpec((down_rows, down_columns), lambda i: (i, int(packs))),
            vector,
        ],
        [columns, columns, fixed(rows, width), fixed(rows, width), vector],
        [
            shape((rows, hidden), BF),
            shape((rows, hidden), BF),
            shape((rows, width), dtype),
            shape((rows, width), dtype),
            shape((1, hidden), F32),
        ],
        8 * rows * width * hidden,
        4 * width * hidden + rows * (4 * hidden + 8 * width),
        2 * rows * hidden,
        [pltpu.VMEM((rows, width), F32)] * 2,
    )(x, og, up, down, bias)


def up_grad_kernel(count, *refs):
    xs, pres, (_, out_ref) = refs[:count], refs[count : 2 * count], refs[2 * count :]
    out_ref[...] = functools.reduce(jnp.add, [mm(x[...], p[...], TN) for x, p in zip(xs, pres)]).astype(BF)


def down_grad_kernel(owned, count, *refs):
    acts, ogs, out_ref = refs[:count], refs[count : 2 * count], refs[2 * count]
    grad = functools.reduce(jnp.add, [mm(a[...], g[...], TN) for a, g in zip(acts, ogs)]).astype(BF)
    width = grad.shape[1]
    parts = out_ref.shape[1] // width
    for f in range(out_ref.shape[0] // owned):
        for j in range(parts):
            start = (f * parts + j) * owned
            out_ref[f * owned : (f + 1) * owned, j * width : (j + 1) * width] = grad[start : start + owned, :]


def down_grad(acts, ogs, owned, block=256):
    count, (rows, hidden), width = len(acts), acts[0].shape, ogs[0].shape[1]
    steps = width // block
    return call(
        functools.partial(down_grad_kernel, owned, count),
        (steps,),
        [pl.BlockSpec((rows, hidden // steps), lambda i: (0, i))] * count + [fixed(rows, width)] * count,
        pl.BlockSpec((block, hidden), lambda i: (i, 1)),
        shape((width, 2 * hidden), BF),
        2 * count * rows * width * hidden,
        2 * count * rows * (width + hidden) + 2 * width * hidden,
    )(*acts, *ogs)


def up_grad(xs, pres, packed, block=256):
    count, (rows, width), hidden = len(xs), xs[0].shape, pres[0].shape[1]
    return pl.pallas_call(
        functools.partial(up_grad_kernel, count),
        grid=(width // block,),
        in_specs=[pl.BlockSpec((rows, block), lambda i: (0, i))] * count
        + [fixed(rows, hidden)] * count
        + [pl.BlockSpec(memory_space=pl.ANY)],
        out_specs=pl.BlockSpec((block, hidden), lambda i: (i, 0)),
        out_shape=shape((width, 2 * hidden), BF),
        input_output_aliases={2 * count: 0},
        compiler_params=pltpu.CompilerParams(vmem_limit_bytes=VMEM_BYTES),
        cost_estimate=pl.CostEstimate(
            flops=2 * count * rows * width * hidden,
            bytes_accessed=2 * count * rows * (width + hidden) + 2 * width * hidden,
            transcendentals=0,
        ),
    )(*xs, *pres, packed)


def deal(here, part, keep_ref, send_ref, at):
    rows, n = keep_ref.shape[1], part.shape[1]
    first = here[2] == 0
    for q in range(keep_ref.shape[0]):
        top, low = part[2 * q * rows : (2 * q + 1) * rows], part[(2 * q + 1) * rows : (2 * q + 2) * rows]
        keep_ref[q, :, at : at + n] = jnp.where(first, top, low)
        send_ref[q, :, at : at + n] = jnp.where(first, low, top)


def out_grad_kernel(group, per_part, here, *refs):
    atts, (branch_ref, keep_ref, send_ref) = refs[:group], refs[group:]
    owner = lax.div(pl.program_id(0), per_part)
    att = pick([a[...] for a in atts], lax.rem(owner - here[3] + group, group))
    deal(here, mm(att, branch_ref[...], TN).astype(BF), keep_ref, send_ref, 0)


def project_out_grad(here, lines, atts, branch, block=256):
    rows, depth = branch.shape
    group = len(atts)
    owned = depth // (2 * lines.chips)
    block = min(block, depth // group)
    per_part = depth // group // block
    out = pl.BlockSpec((block // (2 * owned), owned, depth), lambda i, h: (i, 0, 0))
    return call(
        functools.partial(out_grad_kernel, group, per_part),
        (depth // block,),
        [pl.BlockSpec((rows, block), lambda i, h: (0, lax.rem(i, per_part)))] * group + [fixed(rows, depth)],
        [out, out],
        [shape((lines.chips, owned, depth), BF)] * 2,
        2 * rows * depth * depth,
        2 * depth * (2 * rows + depth),
        scalars=1,
    )(here, *atts, branch)


def project_grad_kernel(here, x_ref, dq_ref, dk_ref, dv_ref, small_ref, keep_ref, send_ref):
    x, at = x_ref[...], 0
    for ref in (dq_ref, dk_ref, dv_ref):
        deal(here, mm(x, ref[...], TN).astype(BF), keep_ref, send_ref, at)
        at += ref.shape[1]
    deal(here, small_ref[...].T.astype(BF), keep_ref, send_ref, at)


def project_grad(here, lines, x, grads, small, block=512):
    rows, depth = x.shape
    width = grads[0].shape[1]
    owned = depth // (2 * lines.chips)
    columns = 3 * width + SMALL
    cols = lambda i, h: (0, i)
    out = pl.BlockSpec((block // (2 * owned), owned, columns), lambda i, h: (i, 0, 0))
    return call(
        project_grad_kernel,
        (depth // block,),
        [pl.BlockSpec((rows, block), cols)] + [fixed(rows, width)] * 3 + [pl.BlockSpec((SMALL, block), cols)],
        [out, out],
        [shape((lines.chips, owned, columns), BF)] * 2,
        6 * rows * depth * width,
        2 * rows * (depth + 3 * width) + 2 * depth * columns,
        scalars=1,
    )(here, x, *grads, small)


def after(values, *earlier):
    return lax.optimization_barrier((values, earlier))[0]


def on_device(
    lines, tokens, positions, ln1_gain, ln1_bias, qkv_weight, qkv_bias, out_weight, out_bias,
    ln2_gain, ln2_bias, fc1_weight, fc1_bias, fc2_weight, fc2_bias, out_grad,
):
    rows, width = tokens.shape[1], tokens.shape[2]
    depth = qkv_weight.shape[0]
    owners, group = width // depth, lax.axis_size(SEQ)
    side, here = lax.axis_index(SEQ), lines.here()
    others = range(1, group)
    heads = width // group
    hidden_owned = fc2_weight.shape[0] // group
    hidden_width = hidden_owned * owners
    packs = hidden_owned % depth == 0

    def gather(values):
        return lax.all_gather(values, SHARD, axis=0, tiled=True)

    def scatter(values):
        return lax.psum_scatter(values, SHARD, scatter_dimension=0, tiled=True)

    def to_next(values, d):
        return lax.ppermute(values, SEQ, shifted(group, d))

    def spread(values):
        return [values] + [to_next(values, d) for d in others]

    def in_order(parts):
        stacked = jnp.stack(parts)
        return [take(stacked, (k - side) % group, 0) for k in range(group)]

    spots = positions[:, 0, :].astype(BF).reshape(-1)
    lines_of = -(-spots.size // width)
    spots = jnp.pad(spots, (0, -(-lines_of // 16) * 16 * width - spots.size)).reshape(-1, width)
    clip = spread(jnp.concatenate([tokens[0], spots], axis=0))
    places = [v[rows:].reshape(-1)[: 3 * rows].reshape(3, rows).astype(F32) for v in clip]
    tables = rotary_tables(jnp.concatenate(places, axis=1))

    names = (ln1_gain, ln1_bias, out_bias, ln2_gain, ln2_bias, fc2_bias, qkv_bias, fc1_bias)
    counts = [p.size // depth for p in names]
    if packs:
        own_att, own_feed = share(here, group, qkv_weight, fc1_weight, fc2_weight, out_weight, names)
        w_up = w_down = w_out = gather(own_feed)
        out_at = 2 * hidden_width // width
    else:
        own_qkv = take(qkv_weight.reshape(depth, 3, group, heads), side, 2).reshape(depth, 3 * heads)
        extra = jnp.concatenate([p.reshape(-1, depth).T for p in names], axis=1)
        own_att = jnp.concatenate([own_qkv, jnp.pad(extra, ((0, 0), (0, SMALL - sum(counts))))], axis=1)
        own_up = take(fc1_weight.reshape(depth, owners, group, hidden_owned), side, 2).reshape(depth, -1)
        own_down = take(fc2_weight.reshape(group, hidden_owned, width), side, 0)
        w_up, w_down, w_out, out_at = gather(own_up), gather(own_down), gather(out_weight), 0
    qkv_mine, qkv_sib = staged_gather(lines, here, own_att, (tables, clip))
    grads = spread(out_grad[0])

    qkv, w_qkv, normed_one, rows_of = project(here, clip, rows, qkv_mine, qkv_sib, tables, heads)
    vectors, at = [], 0
    for n in counts:
        vectors.append(rows_of[at : at + n].reshape(n, owners, depth).transpose(1, 0, 2).reshape(1, -1))
        at += n
    gain_one, _, b_out, gain_two, bias_two, b_down, _, b_up = vectors
    b_up = take(b_up.reshape(owners, group, hidden_owned), side, 1).reshape(1, -1)
    att, lse = attend(qkv)

    att = after(att, grads)
    atts = [att] + [to_next(att[d * rows : (d + 1) * rows], -d) for d in others]
    hidden, normed_two = project_out(here, atts, w_out, out_at, tokens[0], b_out, gain_two, bias_two)
    normed = spread(normed_two)

    fed = [None] * group
    for d in range(group):
        x = after(normed[d], fed[0][2]) if d else normed[0]
        fed[d] = feed(x, grads[d], w_up, w_down, packs, b_up, depth, F32 if d == 0 else BF)
    acts, pres, dns, outs, sums = zip(*fed)
    dn_far = [to_next(dns[d], -d) for d in others]
    out_far = [to_next(outs[d], -d) for d in others]
    dn_own = dns[0]
    if packs:
        fed_grads = down_grad(acts, grads, depth)
        fed_grads = up_grad(normed, pres, fed_grads)
        dn_own = after(dn_own, fed_grads)
    hidden_grad, branch, sums_two, *shares = hidden_back(
        here, dn_own, dn_far, hidden, out_grad[0], gain_two, w_out, out_at
    )
    if packs:
        fed_sum = scatter(fed_grads)
    att_grads = jnp.concatenate([shares[0]] + [to_next(shares[d], d) for d in others], axis=0)

    out_sum = StagedSum(lines, here, *project_out_grad(here, lines, atts, branch))
    att_grads = after(att_grads, out_sum.short())

    *qkv_grads, sums_qkv = attend_back(qkv, att, lse, att_grads, tables)
    qkv_grads = after(qkv_grads, (out_far, out_sum.arrived))

    own = (jnp.arange(group) == side).astype(F32)
    qkv_b = sums_qkv[:3, None, :] * own[None, :, None]
    up_b = functools.reduce(jnp.add, sums).reshape(owners, 1, hidden_owned) * own[None, :, None]
    vectors = (jnp.zeros((2, width), F32), sums_two[2], sums_two[0], sums_two[1], sums_two[3], qkv_b, up_b)
    rows_of = [vectors[0]]
    rows_of += [v.reshape(owners, n, depth).transpose(1, 0, 2).reshape(n, width) for v, n in zip(vectors[1:], counts[2:])]
    rows_of = jnp.pad(jnp.concatenate(rows_of, axis=0), ((0, SMALL - sum(counts)), (0, 0)))
    qkv_sum = StagedSum(lines, here, *project_grad(here, lines, normed_one, qkv_grads, rows_of))

    back = [None] * group
    before = qkv_sum.keep
    for d in list(others) + [0]:
        back[d] = project_back(after(qkv_grads, before), w_qkv, clip[d], d, rows, F32 if d == 0 else BF)
        if d == group - 1:
            qkv_sum.keep = after(qkv_sum.keep, back[d][0])
            before = qkv_sum.short()
    dn_one, sums_one = zip(*back)
    dn_one_far = [to_next(dn_one[d], -d) for d in others]
    sums_one = functools.reduce(jnp.add, sums_one)
    sums_one = sums_one + lax.ppermute(sums_one, "c", shifted(2, 1))
    sums_one = functools.reduce(
        jnp.add, [sums_one] + [lax.ppermute(sums_one, lines.short, shifted(lines.n_short, d)) for d in range(1, lines.n_short)]
    )
    late = sums_one[:2].reshape(2, lines.outer, lines.inner, 2, depth)
    late = take(take(late, here[2], 3), here[1], 2 if lines.outer_long else 1)
    late = jnp.pad(late.transpose(1, 2, 0), ((0, 0), (0, 0), (0, SMALL - 2)))
    out_sum.arrived = after(out_sum.arrived, before)
    out_sum.long()
    qkv_sum.long((late,))
    tokens_grad = tokens_back(dn_one[0], dn_one_far, tokens[0], hidden_grad, gain_one)
    block_out = hidden + outs[0] + b_down
    for far in out_far:
        block_out = block_out + far.astype(F32)
    block_out = block_out.astype(BF)

    def from_next(values):
        return [values] + [to_next(values, -d) for d in others]

    if packs:
        up_total, down_total = finish_feed(here, from_next(fed_sum), fc1_weight.shape, fc2_weight.shape)
    else:
        up_sum = scatter(functools.reduce(jnp.add, [mm(x, p, TN) for x, p in zip(normed, pres)]).astype(BF))
        down_sum = scatter(functools.reduce(jnp.add, [mm(a, g, TN) for a, g in zip(acts, grads)]).astype(BF))
        shares = [v.reshape(depth, owners, hidden_owned) for v in in_order(from_next(up_sum))]
        up_total = jnp.stack(shares, axis=2).reshape(depth, -1).astype(F32)
        down_total = jnp.concatenate(in_order(from_next(down_sum)), axis=0).astype(F32)
    out_last = out_sum.last()
    qkv_sum.parts = after(qkv_sum.parts, (tokens_grad, block_out, up_total, down_total, out_last))
    att_sums = jnp.concatenate([out_last, qkv_sum.last()], axis=1)
    out_total, qkv_total, g1, b1, bo, g2, b2, bd, bq, bu = finish_attention(here, from_next(att_sums), width, counts)
    return (
        block_out[None], tokens_grad[None], g1, b1, qkv_total, bq, out_total, bo, g2, b2, up_total, bu,
        down_total, bd,
    )


def solution(mesh):
    lines = Lines(mesh)
    vector, matrix, tokens = P(SHARD), P(SHARD, None), P(SHARD, SEQ, None)
    return jax.shard_map(
        functools.partial(on_device, lines),
        mesh=lines.mesh,
        in_specs=(
            tokens, P(None, SHARD, SEQ), vector, vector, matrix, vector, matrix, vector, vector, vector, matrix, vector,
            matrix, vector, tokens,
        ),
        out_specs=(
            tokens, tokens, vector, vector, matrix, vector, matrix, vector, vector, vector, matrix, vector, matrix, vector
        ),
        check_vma=False,
    )
```

```python
import functools

import jax
import jax.numpy as jnp
import numpy as np
from jax import lax
from jax.experimental import pallas as pl
from jax.experimental.pallas import tpu as pltpu
from jax.sharding import Mesh, PartitionSpec as P

HD = 64
EPS = 1e-06
THETA = 10000.0
LOG2E = 1.4426950408889634
SCALE = HD**-0.5
BF = jnp.bfloat16
F32 = jnp.float32
NT = (((1,), (1,)), ((), ()))
TN = (((0,), (0,)), ((), ()))
NN = (((1,), (0,)), ((), ()))
SMALL = 128
VMEM_BYTES = 56 << 20
LOW, HIGH = 0.25, 200
SHARD = ("o", "i", "c")
SEQ = "seq"


def mm(a, b, dims=NN):
    return lax.dot_general(a, b, dims, preferred_element_type=F32)


def shifted(size, by):
    return [(i, (i + by) % size) for i in range(size)]


def take(values, index, axis):
    return lax.dynamic_index_in_dim(values, index, axis, keepdims=False)


def shape(dims, dtype):
    return jax.ShapeDtypeStruct(dims, dtype)


def fixed(*dims):
    return pl.BlockSpec(dims, lambda *_: (0,) * len(dims))


def spec(block, index):
    return pl.BlockSpec(block, index)


def call(kernel, grid, in_specs, out_specs, out_shape, flops, moved, exps=0, scratch=(), scalars=0, weight=LOW):
    return pl.pallas_call(
        kernel,
        grid_spec=pltpu.PrefetchScalarGridSpec(
            num_scalar_prefetch=scalars,
            grid=grid,
            in_specs=in_specs,
            out_specs=out_specs,
            scratch_shapes=list(scratch),
        ),
        out_shape=out_shape,
        compiler_params=pltpu.CompilerParams(vmem_limit_bytes=VMEM_BYTES),
        cost_estimate=pl.CostEstimate(flops=int(weight * flops), bytes_accessed=int(weight * moved), transcendentals=int(weight * exps)),
    )


def pick(parts, index):
    chosen = parts[0]
    for k in range(1, len(parts)):
        chosen = jnp.where(index == k, parts[k], chosen)
    return chosen


def chips_in_line(mesh):
    chips = mesh.devices.shape[0] // 2
    places = [getattr(d, "coords", None) for d in mesh.devices[::2, 0]]
    if places[0] is None or chips < 2:
        return 2 if chips % 2 == 0 else 1
    axis = [a for a in range(3) if places[0][a] != places[1][a]][0]
    inner = 1
    while inner < chips and all(places[inner][a] == places[0][a] for a in range(3) if a != axis):
        inner += 1
    return inner


class Lines:
    def __init__(self, mesh):
        fsdp, seq = mesh.devices.shape
        self.chips = fsdp // 2
        self.inner = chips_in_line(mesh)
        self.outer = self.chips // self.inner
        self.mesh = Mesh(mesh.devices.reshape(self.outer, self.inner, 2, seq), SHARD + (SEQ,))
        self.outer_long = self.outer >= self.inner
        self.long, self.short = ("o", "i") if self.outer_long else ("i", "o")
        self.n_long, self.n_short = max(self.outer, self.inner), min(self.outer, self.inner)

    def place(self, long, short):
        return (long, short) if self.outer_long else (short, long)

    def split(self, values):
        return values.reshape(self.outer, self.inner, *values.shape[1:])

    def here(self):
        return jnp.stack([lax.axis_index(a) for a in (self.long, self.short, "c", SEQ)]).astype(jnp.int32)


def stack_kernel(lines, here, *refs):
    *pieces, out, sems = refs
    copies = []
    for n, piece in enumerate(pieces):
        back_short, back_long = n // lines.n_long, n % lines.n_long
        long = lax.rem(here[0] + (lines.n_long - back_long), lines.n_long)
        short = lax.rem(here[1] + (lines.n_short - back_short), lines.n_short)
        a, b = lines.place(long, short)
        copies.append(pltpu.make_async_copy(piece, out.at[a, b], sems.at[n]))
    for copy in copies:
        copy.start()
    for copy in copies:
        copy.wait()


def staged_gather(lines, here, values, meanwhile):
    line = [values] + [lax.ppermute(values, lines.long, shifted(lines.n_long, d)) for d in range(1, lines.n_long)]
    pieces = list(line)
    for d in range(1, lines.n_short):
        pieces += [lax.ppermute(v, lines.short, shifted(lines.n_short, d)) for v in line]
    dims = (lines.outer, lines.inner) + values.shape
    pieces = after(pieces, meanwhile)
    mine = call(
        functools.partial(stack_kernel, lines),
        (1,),
        [pl.BlockSpec(memory_space=pl.ANY)] * len(pieces),
        pl.BlockSpec(dims, lambda *_: (0,) * 4),
        shape(dims, values.dtype),
        0,
        4 * lines.chips * values.size,
        scratch=[pltpu.SemaphoreType.DMA((len(pieces),))],
        scalars=1,
    )(here, *pieces)
    mine = mine.reshape((lines.chips,) + values.shape)
    return mine, lax.ppermute(mine, "c", shifted(2, 1))


def add_first_kernel(here, keep_ref, got_ref, out_ref):
    out_ref[...] = (keep_ref[...].astype(F32) + got_ref[...].astype(F32)).astype(BF)


def add_second_kernel(lines, late, here, keep_ref, got_ref, *refs):
    ins, refs = refs[: lines.n_short - 1], refs[lines.n_short - 1 :]
    late_ref, outs = (refs[0], refs[1:]) if late else (None, refs)
    for k, out in enumerate(outs):
        at = lines.place(lax.rem(here[0] + k, lines.n_long), 0)
        total = keep_ref[at].astype(F32) + got_ref[at].astype(F32)
        for r in ins:
            total = total + r[at].astype(F32)
        if late:
            n = total.shape[1] - SMALL
            out[:, :n] = total[:, :n].astype(BF)
            out[:, n:] = (total[:, n:] + late_ref[at[0] + at[1]]).astype(BF)
        else:
            out[...] = total.astype(BF)


def add_last_kernel(count, *refs):
    ins, beside, out = refs[:count], refs[count:-1], refs[-1]
    at = 0
    for ref in beside:
        out[:, at : at + ref.shape[1]] = ref[...]
        at += ref.shape[1]
    out[:, at:] = functools.reduce(jnp.add, [r[...].astype(F32) for r in ins]).astype(BF)


class StagedSum:
    def __init__(self, lines, here, keep, send):
        self.lines, self.here = lines, here
        self.got = lines.split(lax.ppermute(send, "c", shifted(2, 1)))
        self.keep = lines.split(keep)
        self.rows, self.columns = keep.shape[1:]
        self.dims = lines.place(lines.n_long, 1) + (self.rows, self.columns)
        self.size = lines.n_long * self.rows * self.columns

    def across(self, d):
        lines = self.lines
        return pl.BlockSpec(self.dims, lambda i, h: lines.place(0, lax.rem(h[1] + d, lines.n_short)) + (0, 0))

    def short(self):
        lines, dims = self.lines, self.dims
        away = [
            call(
                add_first_kernel,
                (1,),
                [self.across(d)] * 2,
                pl.BlockSpec(dims, lambda i, h: (0, 0, 0, 0)),
                shape(dims, BF),
                self.size,
                6 * self.size,
                scalars=1,
            )(self.here, self.keep, self.got)
            for d in range(1, lines.n_short)
        ]
        self.arrived = [lax.ppermute(v, lines.short, shifted(lines.n_short, d + 1)) for d, v in enumerate(away)]
        return away

    def long(self, late=()):
        lines = self.lines
        flat = pl.BlockSpec((self.rows, self.columns), lambda i, h: (0, 0))
        parts = call(
            functools.partial(add_second_kernel, lines, len(late) > 0),
            (1,),
            [self.across(0)] * 2
            + [pl.BlockSpec(self.dims, lambda i, h: (0, 0, 0, 0))] * len(self.arrived)
            + [fixed(*v.shape) for v in late],
            [flat] * lines.n_long,
            [shape((self.rows, self.columns), BF)] * lines.n_long,
            3 * self.size,
            8 * self.size,
            scalars=1,
        )(self.here, self.keep, self.got, *self.arrived, *late)
        self.parts = [parts[0]]
        self.parts += [lax.ppermute(parts[d], lines.long, shifted(lines.n_long, d)) for d in range(1, lines.n_long)]
        return parts

    def last(self, beside=()):
        columns = self.columns + sum(v.shape[1] for v in beside)
        return call(
            functools.partial(add_last_kernel, len(self.parts)),
            (1,),
            [fixed(self.rows, self.columns)] * len(self.parts) + [fixed(*v.shape) for v in beside],
            fixed(self.rows, columns),
            shape((self.rows, columns), BF),
            self.size,
            3 * self.size,
        )(*self.parts, *beside)


def share_kernel(group, here, qkv_ref, up_ref, down_ref, out_ref, *refs):
    *small_refs, att_ref, feed_ref = refs
    side = here[3]
    depth, width = out_ref.shape
    heads = width // group
    for k in range(3):
        parts = [qkv_ref[:, k * width + g * heads : k * width + (g + 1) * heads] for g in range(group)]
        att_ref[:, k * heads : (k + 1) * heads] = pick(parts, side)
    rows = [r[j : j + depth].astype(F32).reshape(1, depth) for r in small_refs for j in range(0, r.shape[0], depth)]
    rows.append(jnp.zeros((SMALL - len(rows), depth), F32))
    att_ref[:, 3 * heads :] = jnp.concatenate(rows, axis=0).T.astype(BF)
    owned = down_ref.shape[0] // group
    hidden = up_ref.shape[1] // group
    for f in range(hidden // owned):
        parts = [up_ref[:, (f * group + g) * owned : (f * group + g + 1) * owned] for g in range(group)]
        feed_ref[:, f * owned : (f + 1) * owned] = pick(parts, side)
    for j in range(owned // depth):
        parts = [down_ref[g * owned + j * depth : g * owned + (j + 1) * depth, :] for g in range(group)]
        feed_ref[:, hidden + j * width : hidden + (j + 1) * width] = pick(parts, side)
    feed_ref[:, 2 * hidden :] = out_ref[...]


def share(here, group, qkv, up, down, out, small):
    depth, width = out.shape
    args = (qkv, up, down, out, *small)
    att, feed_columns = qkv.shape[1] // group + SMALL, 2 * up.shape[1] // group + width
    return call(
        functools.partial(share_kernel, group),
        (1,),
        [fixed(*a.shape) for a in args],
        [fixed(depth, att), fixed(depth, feed_columns)],
        [shape((depth, att), BF), shape((depth, feed_columns), BF)],
        0,
        8 * depth * (att + feed_columns),
        scalars=1,
    )(here, *args)


def finish_attention_kernel(group, here, *refs):
    shares, (out_ref, qkv_ref, *vector_refs) = refs[:group], refs[group:]
    width = out_ref.shape[1]
    heads = width // group
    total = functools.reduce(jnp.add, [r[:, :width].astype(F32) for r in shares])
    out_ref[...] = total
    small = functools.reduce(jnp.add, [r[:, -SMALL:].astype(F32) for r in shares])
    small, row = small.T, 0
    for ref in vector_refs:
        for at in range(0, ref.shape[0], small.shape[1]):
            ref[at : at + small.shape[1]] = small[row]
            row += 1
    for k in range(group):
        source = lax.rem(k - here[3] + group, group)
        for m in range(3):
            at, start = m * width + k * heads, width + m * heads
            parts = [r[:, start : start + heads] for r in shares]
            qkv_ref[:, at : at + heads] = pick(parts, source).astype(F32)


def finish_attention(here, shares, width, counts):
    depth, group = shares[0].shape[0], len(shares)
    return call(
        functools.partial(finish_attention_kernel, group),
        (1,),
        [fixed(*v.shape) for v in shares],
        [fixed(depth, width), fixed(depth, 3 * width)] + [fixed(n * depth) for n in counts],
        [shape((depth, width), F32), shape((depth, 3 * width), F32)] + [shape((n * depth,), F32) for n in counts],
        0,
        24 * depth * width,
        scalars=1,
    )(here, *shares)


def finish_feed_kernel(group, here, *refs):
    shares, (up_ref, down_ref) = refs[:group], refs[group:]
    depth, width = shares[0].shape[0], down_ref.shape[1]
    owned = down_ref.shape[0] // group
    hidden = up_ref.shape[1] // group
    for k in range(group):
        source = lax.rem(k - here[3] + group, group)
        for f in range(hidden // owned):
            at = (f * group + k) * owned
            up_ref[:, at : at + owned] = pick([r[:, f * owned : (f + 1) * owned] for r in shares], source).astype(F32)
        for j in range(owned // depth):
            at, start = k * owned + j * depth, hidden + j * width
            down_ref[at : at + depth, :] = pick([r[:, start : start + width] for r in shares], source).astype(F32)


def finish_feed(here, shares, up_shape, down_shape):
    return call(
        functools.partial(finish_feed_kernel, len(shares)),
        (1,),
        [fixed(*v.shape) for v in shares],
        [fixed(*up_shape), fixed(*down_shape)],
        [shape(up_shape, F32), shape(down_shape, F32)],
        0,
        12 * up_shape[0] * up_shape[1],
        scalars=1,
    )(here, *shares)


def rotated(values, cos, low, high):
    half = 2 * (HD // 3 // 2) // 2
    return values * cos + pltpu.roll(values, values.shape[1] - half, 1) * low + pltpu.roll(values, half, 1) * high


def project_kernel(group, here, *refs):
    clip, refs = refs[:group], refs[group:]
    mine_ref, sib_ref, mine_small, sib_small, cos_ref, low_ref, high_ref, out_ref, w_ref, x_ref, lines_ref, bias = refs
    rows = mine_ref.shape[1]
    core, side, step = here[2], here[3], pl.program_id(0)
    width = out_ref.shape[1]

    @pl.when(step == 0)
    def _():
        owners = []
        for q in range(mine_small.shape[0]):
            a, b = mine_small[q].astype(F32), sib_small[q].astype(F32)
            owners += [jnp.where(core == 0, a, b), jnp.where(core == 0, b, a)]
        lines = jnp.concatenate(owners, axis=0).T[: lines_ref.shape[0]]
        lines_ref[...] = lines
        count = width // rows
        for k in range(3):
            for j in range(count):
                at = [(k * group + g) * count + j for g in range(group)]
                parts = [lines[6 + p % 3 : 7 + p % 3, p // 3 * rows : (p // 3 + 1) * rows] for p in at]
                bias[k : k + 1, j * rows : (j + 1) * rows] = pick(parts, side)
        tokens = clip[0].shape[0]
        block = min(256, tokens)
        for d, ref in enumerate(clip):
            for r in range(0, tokens, block):
                normal, _ = normalise(ref[r : r + block, :].astype(F32))
                at = d * tokens + r
                x_ref[at : at + block, :] = (normal * lines[0:1] + lines[1:2]).astype(BF)

    for q in range(mine_ref.shape[0]):
        w_ref[pl.ds(pl.multiple_of((2 * q + core) * rows, rows), rows), :] = mine_ref[q]
        w_ref[pl.ds(pl.multiple_of((2 * q + 1 - core) * rows, rows), rows), :] = sib_ref[q]
    values = mm(x_ref[...], w_ref[...]) + bias[pl.ds(step, 1), :]

    @pl.when(step < 2)
    def _():
        cos, low, high = cos_ref[...], low_ref[...], high_ref[...]
        for j in range(0, width, 128):
            out_ref[:, j : j + 128] = rotated(values[:, j : j + 128], cos, low, high).astype(BF)

    @pl.when(step >= 2)
    def _():
        out_ref[...] = values.astype(BF)


def project(here, clip, tokens, mine, sib, tables, width):
    depth, group = clip[0].shape[1], len(clip)
    rows = tokens * group
    part = pl.BlockSpec(mine.shape[:2] + (width,), lambda i, h: (0, 0, i))
    small = pl.BlockSpec(mine.shape[:2] + (SMALL,), lambda i, h: (0, 0, 3 * width // SMALL))
    return call(
        functools.partial(project_kernel, group),
        (3,),
        [fixed(tokens, depth)] * group + [part, part, small, small] + [fixed(rows, 128)] * 3,
        [
            pl.BlockSpec((rows, width), lambda i, h: (0, i)),
            pl.BlockSpec((depth, width), lambda i, h: (0, i)),
            fixed(rows, depth),
            fixed(16, depth),
        ],
        [shape((rows, 3 * width), BF), shape((depth, 3 * width), BF), shape((rows, depth), BF), shape((16, depth), F32)],
        6 * rows * depth * width,
        12 * depth * width + 2 * rows * (depth + 3 * width),
        scratch=[pltpu.VMEM((8, width), F32)],
        scalars=1,
    )(here, *clip, mine, sib, mine, sib, *tables)


def rotary_tables(positions):
    width = 2 * (HD // 3 // 2)
    half = width // 2
    freqs = np.power(np.float32(THETA), -(np.arange(half, dtype=np.float32) * np.float32(2.0 / width)))
    column = np.arange(2 * HD) % HD
    turns = column < 3 * width
    axis = np.minimum(column // width, 2)
    freq = np.where(turns, freqs[column % half], 0.0).astype(np.float32)
    leading = turns & (column % width < half)
    trailing = turns & (column % width >= half)
    place = jnp.where(axis == 0, positions[0][:, None], jnp.where(axis == 1, positions[1][:, None], positions[2][:, None]))
    angle = place * freq
    sine = jnp.sin(angle)
    return jnp.cos(angle), jnp.where(leading, -sine, 0.0), jnp.where(trailing, sine, 0.0)


def over_blocks(rows, block, step):
    if rows // block <= 4:
        for i in range(rows // block):
            step(pl.ds(i * block, block))
    else:

        def body(i, carry):
            step(pl.ds(pl.multiple_of(i * block, block), block))
            return carry

        lax.fori_loop(0, rows // block, body, 0)


def attend_kernel(block, q_ref, k_ref, v_ref, o_ref, lse_ref):
    rows = q_ref.shape[0]
    first = lax.broadcasted_iota(jnp.int32, (1, 128), 1) < HD
    masks = (first, jnp.logical_not(first))
    factor = jnp.float32(SCALE * LOG2E)
    zero, one = jnp.zeros((), BF), jnp.ones((), BF)

    def scores_of(rs, h):
        return mm(jnp.where(masks[h], q_ref[rs, :], zero), k_ref[...], NT)

    def finish(scores, h):
        peak = jnp.max(scores, axis=1, keepdims=True) * factor
        weights = jnp.exp2(scores * factor - peak).astype(BF)
        out = mm(weights, jnp.where(masks[h], v_ref[...], one))
        total = out[:, (1 - h) * HD : (1 - h) * HD + 1]
        return out * (1.0 / total), peak + jnp.log2(total)

    def store(rs, left, right):
        o_ref[rs, :] = jnp.where(first, left[0], right[0]).astype(BF)
        lse_ref[rs, :] = jnp.where(first, left[1], right[1])

    if rows // block <= 4:
        places = [pl.ds(i * block, block) for i in range(rows // block)]
        turns = [(rs, h) for rs in places for h in range(2)]
        scores, done = scores_of(*turns[0]), []
        for n, (rs, h) in enumerate(turns):
            ahead = scores_of(*turns[n + 1]) if n + 1 < len(turns) else None
            done.append(finish(scores, h))
            if h == 1:
                store(rs, *done[-2:])
            scores = ahead
    else:
        over_blocks(rows, block, lambda rs: store(rs, *[finish(scores_of(rs, h), h) for h in range(2)]))


def attend_back_kernel(
    block, q_ref, k_ref, v_ref, o_ref, lse_ref, do_ref, cos_ref, low_ref, high_ref, dq_ref, dk_ref, dv_ref, sums_ref, dk_sum, dv_sum
):
    rows = q_ref.shape[0]
    first = lax.broadcasted_iota(jnp.int32, (1, 128), 1) < HD
    masks = (first, jnp.logical_not(first))
    factor = jnp.float32(SCALE * LOG2E)
    zero = jnp.zeros((), BF)
    dk_sum[...] = jnp.zeros_like(dk_sum)
    dv_sum[...] = jnp.zeros_like(dv_sum)

    def step(rs):
        q, do = q_ref[rs, :], do_ref[rs, :]
        od = (o_ref[rs, :].astype(F32) * do.astype(F32)).T
        lse = lse_ref[rs, :].T
        dq = None
        for h, mine in enumerate(masks):
            qh, doh, k = jnp.where(mine, q, zero), jnp.where(mine, do, zero), k_ref[...]
            delta = jnp.sum(od[h * HD : (h + 1) * HD, :], axis=0, keepdims=True)
            p = jnp.exp2(mm(k, qh, NT) * factor - lse[h * HD : h * HD + 1, :])
            ds = (p * (mm(v_ref[...], doh, NT) - delta)).astype(BF)
            dv_sum[...] += mm(p.astype(BF), doh)
            dk_sum[...] += mm(ds, qh)
            part = mm(jnp.where(mine, k, zero), ds, TN)
            dq = part if dq is None else dq + part
        dq = (dq.T * SCALE).astype(BF).astype(F32)
        dq_ref[rs, :] = rotated(dq, cos_ref[rs, :], -low_ref[rs, :], -high_ref[rs, :]).astype(BF)

    over_blocks(rows, block, step)
    dk = (dk_sum[...] * SCALE).astype(BF).astype(F32)
    dk_ref[...] = rotated(dk, cos_ref[...], -low_ref[...], -high_ref[...]).astype(BF)
    dv_ref[...] = dv_sum[...].astype(BF)
    sums = [jnp.sum(r[...].astype(F32), axis=0, keepdims=True) for r in (dq_ref, dk_ref, dv_ref)]
    sums_ref[...] = jnp.concatenate(sums + [jnp.zeros((5, 128), F32)], axis=0)


def pair_spec(rows, first=0):
    return pl.BlockSpec((rows, 128), lambda i: (0, first + i))


def attend(qkv, block=512):
    rows, columns = qkv.shape[0], qkv.shape[1] // 3
    pairs = columns // 128
    return call(
        functools.partial(attend_kernel, min(block, (1 << 19) // rows)),
        (pairs,),
        [pair_spec(rows, k * pairs) for k in range(3)],
        [pair_spec(rows)] * 2,
        [shape((rows, columns), BF), shape((rows, columns), F32)],
        16 * rows * rows * columns,
        rows * columns * 12,
        rows * rows * columns // HD,
    )(qkv, qkv, qkv)


def attend_back(qkv, o, lse, do, tables, block=512):
    rows, columns = o.shape
    pairs = columns // 128
    return call(
        functools.partial(attend_back_kernel, min(block, (1 << 19) // rows)),
        (pairs,),
        [pair_spec(rows, k * pairs) for k in range(3)] + [pair_spec(rows)] * 3 + [fixed(rows, 128)] * 3,
        [pair_spec(rows)] * 3 + [pl.BlockSpec((8, 128), lambda i: (0, i))],
        [shape((rows, columns), BF)] * 3 + [shape((8, columns), F32)],
        40 * rows * rows * columns,
        rows * columns * 20,
        rows * rows * columns // HD,
        [pltpu.VMEM((rows, 128), F32)] * 2,
    )(qkv, qkv, qkv, o, lse, do, *tables)


def normalise(values):
    center = values - jnp.mean(values, axis=-1, keepdims=True)
    factor = lax.rsqrt(jnp.mean(center * center, axis=-1, keepdims=True) + EPS)
    return center * factor, factor


def normalise_back(grads, gain, normal, factor):
    e = grads * gain
    inner = e - jnp.mean(e, axis=-1, keepdims=True) - normal * jnp.mean(e * normal, axis=-1, keepdims=True)
    return factor * inner


def column_sums(out_ref, *parts):
    sums = [jnp.sum(p, axis=0, keepdims=True) for p in parts]
    sums.append(jnp.zeros((8 - len(sums), sums[0].shape[1]), F32))
    block = jnp.concatenate(sums, axis=0)

    @pl.when(pl.program_id(0) == 0)
    def _():
        out_ref[...] = block

    @pl.when(pl.program_id(0) > 0)
    def _():
        out_ref[...] += block


def out_kernel(group, here, *refs):
    atts, weights, (tokens_ref, b_ref, gain_ref, bias_ref, hidden_ref, normed_ref) = (
        refs[:group],
        refs[group : 2 * group],
        refs[2 * group :],
    )
    hidden = tokens_ref[...].astype(F32) + b_ref[...]
    for att, w in zip(atts, weights):
        hidden = hidden + mm(att[...], w[...])
    hidden_ref[...] = hidden
    normed_ref[...] = (normalise(hidden)[0] * gain_ref[...] + bias_ref[...]).astype(BF)


def project_out(here, atts, weight, at, tokens, b, gain, bias, block=256):
    rows, width = tokens.shape
    group, heads = len(atts), atts[0].shape[1]
    row = pl.BlockSpec((block, width), lambda i, h: (i, 0))
    return call(
        functools.partial(out_kernel, group),
        (rows // block,),
        [pl.BlockSpec((block, heads), lambda i, h: (i, 0))] * group
        + [pl.BlockSpec((heads, width), lambda i, h, d=d: (lax.rem(h[3] + d, group), at)) for d in range(group)]
        + [row]
        + [fixed(1, width)] * 3,
        [row, row],
        [shape((rows, width), F32), shape((rows, width), BF)],
        2 * rows * width * width,
        2 * width * width + 10 * rows * width,
        scalars=1,
    )(here, *atts, *[weight] * group, tokens, b, gain, bias)


def hidden_back_kernel(group, here, *refs):
    dn_ref, far_refs, (hidden_ref, og_ref, gain_ref, w_ref, grad_ref, branch_ref, sums_ref, *att_refs) = (
        refs[0],
        refs[1:group],
        refs[group:],
    )
    dn = dn_ref[...]
    for far in far_refs:
        dn = dn + far[...].astype(F32)
    normal, factor = normalise(hidden_ref[...])
    og = og_ref[...].astype(F32)
    grad = og + normalise_back(dn, gain_ref[...], normal, factor)
    grad_ref[...] = grad
    branch = grad.astype(BF)
    branch_ref[...] = branch
    att = mm(branch, w_ref[...], NT).astype(BF)
    heads = att.shape[1] // group
    parts = [att[:, k * heads : (k + 1) * heads] for k in range(group)]
    for d, ref in enumerate(att_refs):
        ref[...] = pick(parts, lax.rem(here[3] + d, group))
    column_sums(sums_ref, dn * normal, dn, branch.astype(F32), og)


def hidden_back(here, dn, dn_far, hidden, og, gain, weight, at, block=128):
    rows, width = hidden.shape
    group = 1 + len(dn_far)
    row = pl.BlockSpec((block, width), lambda i, h: (i, 0))
    share = pl.BlockSpec((block, width // group), lambda i, h: (i, 0))
    return call(
        functools.partial(hidden_back_kernel, group),
        (rows // block,),
        [row] * group + [row, row, fixed(1, width), pl.BlockSpec((width, width), lambda i, h: (0, at))],
        [row, row, fixed(8, width)] + [share] * group,
        [shape((rows, width), F32), shape((rows, width), BF), shape((8, width), F32)]
        + [shape((rows, width // group), BF)] * group,
        2 * rows * width * width,
        2 * width * width + 18 * rows * width,
        scalars=1,
        weight=HIGH,
    )(here, dn, *dn_far, hidden, og, gain, weight)


def tokens_back_kernel(extra, *refs):
    dn_ref, far_refs, (tokens_ref, grad_ref, gain_ref, out_ref) = refs[0], refs[1 : 1 + extra], refs[1 + extra :]
    dn = dn_ref[...]
    for far in far_refs:
        dn = dn + far[...].astype(F32)
    normal, factor = normalise(tokens_ref[...].astype(F32))
    out_ref[...] = grad_ref[...] + normalise_back(dn, gain_ref[...], normal, factor)


def tokens_back(dn, dn_far, tokens, grad, gain, block=256):
    rows, width = tokens.shape
    row = pl.BlockSpec((block, width), lambda i: (i, 0))
    return call(
        functools.partial(tokens_back_kernel, len(dn_far)),
        (rows // block,),
        [row] * (3 + len(dn_far)) + [fixed(1, width)],
        row,
        shape((rows, width), F32),
        20 * rows * width,
        14 * rows * width,
    )(dn, *dn_far, tokens, grad, gain)


def project_back_kernel(dq_ref, dk_ref, dv_ref, w_ref, tokens_ref, out_ref, sums_ref):
    width = dq_ref.shape[1]
    total = functools.reduce(
        jnp.add,
        [mm(g[...], w_ref[:, k * width : (k + 1) * width], NT) for k, g in enumerate((dq_ref, dk_ref, dv_ref))],
    )
    out_ref[...] = total.astype(out_ref.dtype)
    normal, _ = normalise(tokens_ref[...].astype(F32))
    column_sums(sums_ref, total * normal, total)


def project_back(grads, weight, tokens, piece, rows, dtype):
    width, depth = grads[0].shape[1], tokens.shape[1]
    block = rows // 2
    row = pl.BlockSpec((block, depth), lambda i: (i, 0))
    return call(
        project_back_kernel,
        (2,),
        [pl.BlockSpec((block, width), lambda i: (2 * piece + i, 0))] * 3 + [fixed(depth, 3 * width), row],
        [row, fixed(8, depth)],
        [shape((rows, depth), dtype), shape((8, depth), F32)],
        6 * rows * width * depth,
        6 * width * depth + rows * (6 * width + 6 * depth),
    )(*grads, weight, tokens)


def unpack_down(block, rows, width):
    parts = block.shape[1] // width
    if parts == 1:
        return block
    owners = block.shape[0] // rows
    return jnp.concatenate(
        [block[f * rows : (f + 1) * rows, j * width : (j + 1) * width] for f in range(owners) for j in range(parts)], axis=0
    )


def feed_kernel(owned, x_ref, og_ref, up_ref, down_ref, b_ref, act_ref, pre_ref, dn_ref, out_ref, sums_ref, dn_sum, out_sum):
    step, last = pl.program_id(0), pl.num_programs(0) - 1
    width = x_ref.shape[1]
    up = up_ref[...]
    down = unpack_down(down_ref[...], owned, width)
    u = mm(x_ref[...], up) + b_ref[...]
    phi = 0.5 * (1.0 + lax.erf(u * 0.7071067811865476))
    slope = phi + u * jnp.exp(-0.5 * u * u) * 0.3989422804014327
    act = (u * phi).astype(BF)
    act_ref[...] = act
    pre = (mm(og_ref[...], down, NT) * slope).astype(BF)
    pre_ref[...] = pre
    sums_ref[...] = jnp.sum(pre.astype(F32), axis=0, keepdims=True)
    dn = mm(pre, up, NT)
    out = mm(act, down)

    @pl.when(step == 0)
    def _():
        dn_sum[...] = dn
        out_sum[...] = out

    @pl.when(step > 0)
    def _():
        dn_sum[...] += dn
        out_sum[...] += out

    @pl.when(step == last)
    def _():
        dn_ref[...] = dn_sum[...].astype(dn_ref.dtype)
        out_ref[...] = out_sum[...].astype(out_ref.dtype)


def feed(x, og, up, down, packs, bias, owned, dtype, block=512):
    rows, width = x.shape
    hidden = bias.shape[1]
    block = min(block, hidden)
    steps = hidden // block
    down_rows = down.shape[0] // steps
    down_columns = hidden if packs else width
    columns = pl.BlockSpec((rows, block), lambda i: (0, i))
    vector = pl.BlockSpec((1, block), lambda i: (0, i))
    return call(
        functools.partial(feed_kernel, owned),
        (steps,),
        [
            fixed(rows, width),
            fixed(rows, width),
            pl.BlockSpec((width, block), lambda i: (0, i)),
            pl.BlockSpec((down_rows, down_columns), lambda i: (i, int(packs))),
            vector,
        ],
        [columns, columns, fixed(rows, width), fixed(rows, width), vector],
        [
            shape((rows, hidden), BF),
            shape((rows, hidden), BF),
            shape((rows, width), dtype),
            shape((rows, width), dtype),
            shape((1, hidden), F32),
        ],
        8 * rows * width * hidden,
        4 * width * hidden + rows * (4 * hidden + 8 * width),
        2 * rows * hidden,
        [pltpu.VMEM((rows, width), F32)] * 2,
    )(x, og, up, down, bias)


def up_grad_kernel(count, *refs):
    xs, pres, (_, out_ref) = refs[:count], refs[count : 2 * count], refs[2 * count :]
    out_ref[...] = functools.reduce(jnp.add, [mm(x[...], p[...], TN) for x, p in zip(xs, pres)]).astype(BF)


def down_grad_kernel(owned, count, *refs):
    acts, ogs, out_ref = refs[:count], refs[count : 2 * count], refs[2 * count]
    grad = functools.reduce(jnp.add, [mm(a[...], g[...], TN) for a, g in zip(acts, ogs)]).astype(BF)
    width = grad.shape[1]
    parts = out_ref.shape[1] // width
    for f in range(out_ref.shape[0] // owned):
        for j in range(parts):
            start = (f * parts + j) * owned
            out_ref[f * owned : (f + 1) * owned, j * width : (j + 1) * width] = grad[start : start + owned, :]


def down_grad(acts, ogs, owned, block=256):
    count, (rows, hidden), width = len(acts), acts[0].shape, ogs[0].shape[1]
    steps = width // block
    return call(
        functools.partial(down_grad_kernel, owned, count),
        (steps,),
        [pl.BlockSpec((rows, hidden // steps), lambda i: (0, i))] * count + [fixed(rows, width)] * count,
        pl.BlockSpec((block, hidden), lambda i: (i, 1)),
        shape((width, 2 * hidden), BF),
        2 * count * rows * width * hidden,
        2 * count * rows * (width + hidden) + 2 * width * hidden,
    )(*acts, *ogs)


def up_grad(xs, pres, packed, block=256):
    count, (rows, width), hidden = len(xs), xs[0].shape, pres[0].shape[1]
    return pl.pallas_call(
        functools.partial(up_grad_kernel, count),
        grid=(width // block,),
        in_specs=[pl.BlockSpec((rows, block), lambda i: (0, i))] * count
        + [fixed(rows, hidden)] * count
        + [pl.BlockSpec(memory_space=pl.ANY)],
        out_specs=pl.BlockSpec((block, hidden), lambda i: (i, 0)),
        out_shape=shape((width, 2 * hidden), BF),
        input_output_aliases={2 * count: 0},
        compiler_params=pltpu.CompilerParams(vmem_limit_bytes=VMEM_BYTES),
        cost_estimate=pl.CostEstimate(
            flops=2 * count * rows * width * hidden,
            bytes_accessed=2 * count * rows * (width + hidden) + 2 * width * hidden,
            transcendentals=0,
        ),
    )(*xs, *pres, packed)


def deal(here, part, keep_ref, send_ref, at):
    rows, n = keep_ref.shape[1], part.shape[1]
    first = here[2] == 0
    for q in range(keep_ref.shape[0]):
        top, low = part[2 * q * rows : (2 * q + 1) * rows], part[(2 * q + 1) * rows : (2 * q + 2) * rows]
        keep_ref[q, :, at : at + n] = jnp.where(first, top, low)
        send_ref[q, :, at : at + n] = jnp.where(first, low, top)


def out_grad_kernel(group, per_part, here, *refs):
    atts, (branch_ref, keep_ref, send_ref) = refs[:group], refs[group:]
    owner = lax.div(pl.program_id(0), per_part)
    att = pick([a[...] for a in atts], lax.rem(owner - here[3] + group, group))
    deal(here, mm(att, branch_ref[...], TN).astype(BF), keep_ref, send_ref, 0)


def project_out_grad(here, lines, atts, branch, block=256):
    rows, depth = branch.shape
    group = len(atts)
    owned = depth // (2 * lines.chips)
    block = min(block, depth // group)
    per_part = depth // group // block
    out = pl.BlockSpec((block // (2 * owned), owned, depth), lambda i, h: (i, 0, 0))
    return call(
        functools.partial(out_grad_kernel, group, per_part),
        (depth // block,),
        [pl.BlockSpec((rows, block), lambda i, h: (0, lax.rem(i, per_part)))] * group + [fixed(rows, depth)],
        [out, out],
        [shape((lines.chips, owned, depth), BF)] * 2,
        2 * rows * depth * depth,
        2 * depth * (2 * rows + depth),
        scalars=1,
    )(here, *atts, branch)


def project_grad_kernel(here, x_ref, dq_ref, dk_ref, dv_ref, small_ref, keep_ref, send_ref):
    x, at = x_ref[...], 0
    for ref in (dq_ref, dk_ref, dv_ref):
        deal(here, mm(x, ref[...], TN).astype(BF), keep_ref, send_ref, at)
        at += ref.shape[1]
    deal(here, small_ref[...].T.astype(BF), keep_ref, send_ref, at)


def project_grad(here, lines, x, grads, small, block=256):
    rows, depth = x.shape
    width = grads[0].shape[1]
    owned = depth // (2 * lines.chips)
    columns = 3 * width + SMALL
    cols = lambda i, h: (0, i)
    out = pl.BlockSpec((block // (2 * owned), owned, columns), lambda i, h: (i, 0, 0))
    return call(
        project_grad_kernel,
        (depth // block,),
        [pl.BlockSpec((rows, block), cols)] + [fixed(rows, width)] * 3 + [pl.BlockSpec((SMALL, block), cols)],
        [out, out],
        [shape((lines.chips, owned, columns), BF)] * 2,
        6 * rows * depth * width,
        2 * rows * (depth + 3 * width) + 2 * depth * columns,
        scalars=1,
    )(here, x, *grads, small)


def after(values, *earlier):
    return lax.optimization_barrier((values, earlier))[0]


def on_device(
    lines, tokens, positions, ln1_gain, ln1_bias, qkv_weight, qkv_bias, out_weight, out_bias,
    ln2_gain, ln2_bias, fc1_weight, fc1_bias, fc2_weight, fc2_bias, out_grad,
):
    rows, width = tokens.shape[1], tokens.shape[2]
    depth = qkv_weight.shape[0]
    owners, group = width // depth, lax.axis_size(SEQ)
    side, here = lax.axis_index(SEQ), lines.here()
    others = range(1, group)
    heads = width // group
    hidden_owned = fc2_weight.shape[0] // group
    hidden_width = hidden_owned * owners
    packs = hidden_owned % depth == 0

    def gather(values):
        return lax.all_gather(values, SHARD, axis=0, tiled=True)

    def scatter(values):
        return lax.psum_scatter(values, SHARD, scatter_dimension=0, tiled=True)

    def to_next(values, d):
        return lax.ppermute(values, SEQ, shifted(group, d))

    def spread(values):
        return [values] + [to_next(values, d) for d in others]

    def in_order(parts):
        stacked = jnp.stack(parts)
        return [take(stacked, (k - side) % group, 0) for k in range(group)]

    spots = positions[:, 0, :].astype(BF).reshape(-1)
    lines_of = -(-spots.size // width)
    spots = jnp.pad(spots, (0, -(-lines_of // 16) * 16 * width - spots.size)).reshape(-1, width)
    clip = spread(jnp.concatenate([tokens[0], spots], axis=0))
    places = [v[rows:].reshape(-1)[: 3 * rows].reshape(3, rows).astype(F32) for v in clip]
    tables = rotary_tables(jnp.concatenate(places, axis=1))

    names = (ln1_gain, ln1_bias, out_bias, ln2_gain, ln2_bias, fc2_bias, qkv_bias, fc1_bias)
    counts = [p.size // depth for p in names]
    if packs:
        own_att, own_feed = share(here, group, qkv_weight, fc1_weight, fc2_weight, out_weight, names)
        w_up = w_down = w_out = gather(own_feed)
        out_at = 2 * hidden_width // width
    else:
        own_qkv = take(qkv_weight.reshape(depth, 3, group, heads), side, 2).reshape(depth, 3 * heads)
        extra = jnp.concatenate([p.reshape(-1, depth).T for p in names], axis=1)
        own_att = jnp.concatenate([own_qkv, jnp.pad(extra, ((0, 0), (0, SMALL - sum(counts))))], axis=1)
        own_up = take(fc1_weight.reshape(depth, owners, group, hidden_owned), side, 2).reshape(depth, -1)
        own_down = take(fc2_weight.reshape(group, hidden_owned, width), side, 0)
        w_up, w_down, w_out, out_at = gather(own_up), gather(own_down), gather(out_weight), 0
    qkv_mine, qkv_sib = staged_gather(lines, here, own_att, (tables, clip))
    grads = spread(out_grad[0])

    qkv, w_qkv, normed_one, rows_of = project(here, clip, rows, qkv_mine, qkv_sib, tables, heads)
    vectors, at = [], 0
    for n in counts:
        vectors.append(rows_of[at : at + n].reshape(n, owners, depth).transpose(1, 0, 2).reshape(1, -1))
        at += n
    gain_one, _, b_out, gain_two, bias_two, b_down, _, b_up = vectors
    b_up = take(b_up.reshape(owners, group, hidden_owned), side, 1).reshape(1, -1)
    att, lse = attend(qkv)

    att = after(att, grads)
    atts = [att] + [to_next(att[d * rows : (d + 1) * rows], -d) for d in others]
    hidden, normed_two = project_out(here, atts, w_out, out_at, tokens[0], b_out, gain_two, bias_two)
    normed = spread(normed_two)

    fed = [None] * group
    for d in range(group):
        x = after(normed[d], fed[0][2]) if d else normed[0]
        fed[d] = feed(x, grads[d], w_up, w_down, packs, b_up, depth, F32 if d == 0 else BF)
    acts, pres, dns, outs, sums = zip(*fed)
    dn_far = [to_next(dns[d], -d) for d in others]
    out_far = [to_next(outs[d], -d) for d in others]
    dn_own = dns[0]
    if packs:
        fed_grads = down_grad(acts, grads, depth)
        fed_grads = up_grad(normed, pres, fed_grads)
        dn_own = after(dn_own, fed_grads)
    hidden_grad, branch, sums_two, *shares = hidden_back(
        here, dn_own, dn_far, hidden, out_grad[0], gain_two, w_out, out_at
    )
    if packs:
        fed_sum = scatter(fed_grads)
    att_grads = jnp.concatenate([shares[0]] + [to_next(shares[d], d) for d in others], axis=0)

    out_sum = StagedSum(lines, here, *project_out_grad(here, lines, atts, branch))
    att_grads = after(att_grads, out_sum.short())

    *qkv_grads, sums_qkv = attend_back(qkv, att, lse, att_grads, tables)
    qkv_grads = after(qkv_grads, (out_far, out_sum.arrived))

    own = (jnp.arange(group) == side).astype(F32)
    qkv_b = sums_qkv[:3, None, :] * own[None, :, None]
    up_b = functools.reduce(jnp.add, sums).reshape(owners, 1, hidden_owned) * own[None, :, None]
    vectors = (jnp.zeros((2, width), F32), sums_two[2], sums_two[0], sums_two[1], sums_two[3], qkv_b, up_b)
    rows_of = [vectors[0]]
    rows_of += [v.reshape(owners, n, depth).transpose(1, 0, 2).reshape(n, width) for v, n in zip(vectors[1:], counts[2:])]
    rows_of = jnp.pad(jnp.concatenate(rows_of, axis=0), ((0, SMALL - sum(counts)), (0, 0)))
    qkv_sum = StagedSum(lines, here, *project_grad(here, lines, normed_one, qkv_grads, rows_of))

    back = [None] * group
    before = qkv_sum.keep
    for d in list(others) + [0]:
        back[d] = project_back(after(qkv_grads, before), w_qkv, clip[d], d, rows, F32 if d == 0 else BF)
        if d == group - 1:
            qkv_sum.keep = after(qkv_sum.keep, back[d][0])
            before = qkv_sum.short()
    dn_one, sums_one = zip(*back)
    dn_one_far = [to_next(dn_one[d], -d) for d in others]
    sums_one = functools.reduce(jnp.add, sums_one)
    sums_one = sums_one + lax.ppermute(sums_one, "c", shifted(2, 1))
    sums_one = functools.reduce(
        jnp.add, [sums_one] + [lax.ppermute(sums_one, lines.short, shifted(lines.n_short, d)) for d in range(1, lines.n_short)]
    )
    late = sums_one[:2].reshape(2, lines.outer, lines.inner, 2, depth)
    late = take(take(late, here[2], 3), here[1], 2 if lines.outer_long else 1)
    late = jnp.pad(late.transpose(1, 2, 0), ((0, 0), (0, 0), (0, SMALL - 2)))
    out_sum.arrived = after(out_sum.arrived, before)
    qkv_sum.arrived = after(qkv_sum.arrived, out_sum.long())
    ahead = qkv_sum.long((late,))
    tokens_grad = tokens_back(dn_one[0], dn_one_far, tokens[0], hidden_grad, gain_one)
    block_out = hidden + outs[0] + b_down
    for far in out_far:
        block_out = block_out + far.astype(F32)
    block_out = block_out.astype(BF)

    def from_next(values):
        return [values] + [to_next(values, -d) for d in others]

    if packs:
        up_total, down_total = finish_feed(here, from_next(fed_sum), fc1_weight.shape, fc2_weight.shape)
    else:
        up_sum = scatter(functools.reduce(jnp.add, [mm(x, p, TN) for x, p in zip(normed, pres)]).astype(BF))
        down_sum = scatter(functools.reduce(jnp.add, [mm(a, g, TN) for a, g in zip(acts, grads)]).astype(BF))
        shares = [v.reshape(depth, owners, hidden_owned) for v in in_order(from_next(up_sum))]
        up_total = jnp.stack(shares, axis=2).reshape(depth, -1).astype(F32)
        down_total = jnp.concatenate(in_order(from_next(down_sum)), axis=0).astype(F32)
    out_last = out_sum.last()
    qkv_sum.parts = after(qkv_sum.parts, (tokens_grad, block_out, up_total, down_total, out_last))
    att_sums = qkv_sum.last((out_last,))
    out_total, qkv_total, g1, b1, bo, g2, b2, bd, bq, bu = finish_attention(here, from_next(att_sums), width, counts)
    return (
        block_out[None], tokens_grad[None], g1, b1, qkv_total, bq, out_total, bo, g2, b2, up_total, bu,
        down_total, bd,
    )


def solution(mesh):
    lines = Lines(mesh)
    vector, matrix, tokens = P(SHARD), P(SHARD, None), P(SHARD, SEQ, None)
    return jax.shard_map(
        functools.partial(on_device, lines),
        mesh=lines.mesh,
        in_specs=(
            tokens, P(None, SHARD, SEQ), vector, vector, matrix, vector, matrix, vector, vector, vector, matrix, vector,
            matrix, vector, tokens,
        ),
        out_specs=(
            tokens, tokens, vector, vector, matrix, vector, matrix, vector, vector, vector, matrix, vector, matrix, vector
        ),
        check_vma=False,
    )
```
